32 devices in a mesh: gy: 8 (over z, x), gx: 4 (over y, core).
Axes of the slice: x: 2, y: 2, z: 4, core: 2. Of those that a mesh axis runs over, the one named last changes fastest.
Arguments:
- cell_index: int32 [3, 12288], P(None, ('gy', 'gx')), may hold values from 0 to 383, as said below
- offsets: float32 [3, 12288], P(None, ('gy', 'gx')), may hold values from 0 to 1
- charges: float32 [12288], P(('gy', 'gx')), may hold values from -6 to 6
- dipoles: float32 [3, 12288], P(None, ('gy', 'gx')), may hold values from -6 to 6
- block_count: int32 [192], P(('gy', 'gx')), may hold values from 32 to 64, as said below
- shear_cells: int32 [1], replicated, may hold values from 1 to 383
Outputs:
- charge_grad: float32 [12288], P(('gy', 'gx'))
- dipole_grad: float32 [3, 12288], P(None, ('gy', 'gx'))
- position_grad: float32 [3, 12288], P(None, ('gy', 'gx'))
- energy: float32 [1], replicated
The draws below stay inside these ranges and needn't reach their ends.
Inputs may be any that keep to these rules, and one draw needn't show every extreme that they name: `cell_index`: slot s lies in block k = s // 64; block k lies on the device d = k // 6 at gy index d // 4 and gx index d % 4; its atoms have x cells from (d % 4) * 96 + (k % 6) * 16 up to 15 beyond, y cells from (d // 4) * 6 up to 5 beyond, and z cells below 360. The first slot of each block sits at the largest x, y and z cells of that range. Row 0 holds x, row 1 y, row 2 z. The live atoms of a block are its first block_count slots; every device holds a full block.
All inputs are finite; a program needn't handle non-finite values.
Results may differ from the reference program's by a relative error of at most 0.0003.
Values sent between devices are 32-bit elements; how exact they have to be, the bound alone decides.
A program may use at most 128 MiB of HBM per device.

```python
import math
import jax
import jax.numpy as jnp
from jax import lax

NX = 384
NZ = 360
CY = 6
BX = 16
ATOM_BLK = 64
PENCILS = 4
CX = 96
NY = 48
NB = 6
ATOM_DEV = 384
ATOMS = 12288
BLOCKS = 192


def draw_cell_index(key, part):
    key = jax.random.fold_in(key, 11)
    subkeys = jax.random.split(key, 3)
    slots = jnp.arange(ATOMS, dtype=jnp.int32)
    device = slots // ATOM_DEV
    row_y = device // PENCILS
    col_x = device % PENCILS
    block_id = slots % ATOM_DEV // ATOM_BLK
    corner = slots % ATOM_BLK == 0
    pick_x = jnp.where(corner, BX - 1, jax.random.randint(subkeys[0], (ATOMS,), 0, BX, dtype=jnp.int32))
    pick_y = jnp.where(corner, CY - 1, jax.random.randint(subkeys[1], (ATOMS,), 0, CY, dtype=jnp.int32))
    pick_z = jnp.where(corner, NZ - 1, jax.random.randint(subkeys[2], (ATOMS,), 0, NZ, dtype=jnp.int32))
    cell_x = col_x * CX + block_id * BX + pick_x
    cell_y = row_y * CY + pick_y
    cell_z = pick_z
    return jnp.stack([cell_x, cell_y, cell_z])


def draw_block_count(key, part):
    key = jax.random.fold_in(key, 23)
    key_low, key_full = jax.random.split(key)
    counts = jax.random.randint(key_low, (BLOCKS,), ATOM_BLK // 2, ATOM_BLK + 1, dtype=jnp.int32)
    full_block = jax.random.randint(key_full, (BLOCKS // NB,), 0, NB, dtype=jnp.int32)
    blocks_all = jnp.arange(BLOCKS, dtype=jnp.int32)
    is_full = blocks_all % NB == full_block[blocks_all // NB]
    return jnp.where(is_full, ATOM_BLK, counts)


def level_of(stream_key, dims, cuts, low, top_value):
    factor_of, own = 1.0, jax.random.fold_in(stream_key, 6)
    for axis_at, shards_of in cuts:
        heights = jnp.exp(jax.random.uniform(jax.random.fold_in(own, axis_at), (shards_of,), jnp.float32, low / len(cuts), top_value / len(cuts)))
        factor_of = factor_of * jnp.repeat(heights, dims[axis_at] // shards_of).reshape([-1 if axis == axis_at else 1 for axis in range(len(dims))])
    return factor_of


def bell_draw(stream_key, dims, spread, most, pieces=(), kind=jnp.bfloat16):
    drawn = jax.random.normal(stream_key, dims, jnp.float32) * spread
    if len(pieces) > 0:
        drawn = level_of(stream_key, dims, pieces, -0.22, 0.18) * drawn
    return jnp.clip(drawn, min=-most, max=most).astype(kind)


def setup_inputs(seed: int = 0) -> dict:
    seeds = jax.random.split(jax.random.key(seed), 7)
    cell_index = draw_cell_index(jax.random.fold_in(seeds[6], 71), 0)
    offsets = jnp.clip(1.0 * jax.random.uniform(seeds[1], (3, ATOMS), jnp.float32) ** level_of(seeds[1], (3, ATOMS), ((1, 32),), -0.2, 0.2), 0.0, 1.0)
    charges = bell_draw(seeds[2], (ATOMS,), 1.0, 6.0, ((0, 32),), jnp.float32)
    dipoles = bell_draw(seeds[3], (3, ATOMS), 1.0, 6.0, ((1, 32),), jnp.float32)
    block_count = draw_block_count(jax.random.fold_in(seeds[6], 71), 0)
    shear_cells = jax.random.randint(seeds[5], (1,), 1, NX).astype(jnp.int32)
    return {"cell_index": cell_index, "offsets": offsets, "charges": charges, "dipoles": dipoles, "block_count": block_count, "shear_cells": shear_cells}


screening = 0.9
combos = ((0, 0, 0), (1, 0, 0), (0, 1, 0), (0, 0, 1), (2, 0, 0), (0, 2, 0), (0, 0, 2), (1, 1, 0), (1, 0, 1), (0, 1, 1))


def spline_tables(fraction):
    levels = {2: [1.0 - fraction, fraction]}
    current = levels[2]
    for n in range(3, 7):
        inverse_n = 1.0 / (n - 1)
        updated = [None] * n
        updated[n - 1] = inverse_n * fraction * current[n - 2]
        for j in range(1, n - 1):
            updated[n - 1 - j] = inverse_n * ((fraction + j) * current[n - 2 - j] + (n - j - fraction) * current[n - 1 - j])
        updated[0] = inverse_n * (1.0 - fraction) * current[0]
        current = updated
        levels[n] = current
    zero_row = jnp.zeros_like(fraction)

    def entry_at(values_list, k):
        return values_list[k] if 0 <= k < len(values_list) else zero_row

    values_w = jnp.stack(levels[6])
    first_w = jnp.stack([entry_at(levels[5], t - 1) - entry_at(levels[5], t) for t in range(6)])
    second_w = jnp.stack([entry_at(levels[4], t - 2) - 2.0 * entry_at(levels[4], t - 1) + entry_at(levels[4], t) for t in range(6)])
    return jnp.stack([values_w, first_w, second_w])


def spline_modulus(angles):
    return (66.0 + 52.0 * jnp.cos(angles) + 2.0 * jnp.cos(2.0 * angles)) / 120.0


def green_values(index_x, index_y, index_z, shear_step, size_x, size_y, size_z):
    fold_x = (index_x + size_x // 2) % size_x - size_x // 2
    fold_y = (index_y + size_y // 2) % size_y - size_y // 2
    fold_z = (index_z + size_z // 2) % size_z - size_z // 2
    float_x = fold_x.astype(jnp.float32)
    float_z = fold_z.astype(jnp.float32)
    wave_y = fold_y.astype(jnp.float32) + float_x * shear_step.astype(jnp.float32) / size_x
    square_norm = (float_x / size_x) ** 2 + (wave_y / size_y) ** 2 + (float_z / size_z) ** 2
    is_zero = (fold_x == 0) & (fold_y == 0) & (fold_z == 0)
    at_edge = (fold_x == -(size_x // 2)) | (fold_y == -(size_y // 2)) | (fold_z == -(size_z // 2))
    safe_norm = jnp.where(is_zero, 1.0, square_norm)
    moduli = spline_modulus(2.0 * math.pi * float_x / size_x) * spline_modulus(2.0 * math.pi * wave_y / size_y) * spline_modulus(2.0 * math.pi * float_z / size_z)
    kernel = jnp.exp(-((math.pi / screening) ** 2) * safe_norm) / (math.pi * safe_norm * moduli * moduli)
    return jnp.where(is_zero | at_edge, 0.0, kernel)


def reference(cell_index, offsets, charges, dipoles, block_count, shear_cells):
    shear_step = shear_cells[0]
    slots = jnp.arange(ATOMS, dtype=jnp.int32)
    live = (slots % ATOM_BLK < jnp.repeat(block_count, ATOM_BLK, total_repeat_length=ATOMS)).astype(jnp.float32)
    charge_live = charges * live
    dipole_live = dipoles * live[None, :]
    weights = jnp.stack([spline_tables(offsets[a]) for a in range(3)])

    def image_cells(offset_id):
        step_x = offset_id // 36
        step_y = (offset_id // 6) % 6
        step_z = offset_id % 6
        raw_y = cell_index[1] + step_y
        wrapped = raw_y >= NY
        cell_y = jnp.where(wrapped, raw_y - NY, raw_y)
        cell_x = (cell_index[0] + step_x + jnp.where(wrapped, shear_step, 0)) % NX
        cell_z = (cell_index[2] + step_z) % NZ
        return cell_x, cell_y, cell_z, weights[0][:, step_x], weights[1][:, step_y], weights[2][:, step_z]

    def spread_step(grid_now, offset_id):
        cell_x, cell_y, cell_z, weight_x, weight_y, weight_z = image_cells(offset_id)
        amount = (charge_live * weight_x[0] * weight_y[0] * weight_z[0]
                  + dipole_live[0] * weight_x[1] * weight_y[0] * weight_z[0]
                  + dipole_live[1] * weight_x[0] * weight_y[1] * weight_z[0]
                  + dipole_live[2] * weight_x[0] * weight_y[0] * weight_z[1])
        return grid_now.at[cell_x, cell_y, cell_z].add(amount), None

    offset_ids = jnp.arange(216, dtype=jnp.int32)
    spread_grid, _ = lax.scan(spread_step, jnp.zeros((NX, NY, NZ), jnp.float32), offset_ids)

    index_x = jnp.arange(NX, dtype=jnp.int32)
    index_y = jnp.arange(NY, dtype=jnp.int32)
    index_z = jnp.arange(NZ, dtype=jnp.int32)
    fold_x = (index_x + NX // 2) % NX - NX // 2
    tick_count = (fold_x[:, None] * shear_step * index_y[None, :]) % (NX * NY)
    angles = (2.0 * math.pi / (NX * NY)) * tick_count.astype(jnp.float32)
    phases = lax.complex(jnp.cos(angles), -jnp.sin(angles))
    spectrum = jnp.fft.fft(jnp.fft.fft(spread_grid, axis=2), axis=0)
    spectrum = jnp.fft.fft(spectrum * phases[:, :, None], axis=1)
    green_k = green_values(index_x[:, None, None], index_y[None, :, None], index_z[None, None, :], shear_step, NX, NY, NZ)
    energy = 0.5 / (NX * NY * NZ) * jnp.sum(green_k * (jnp.real(spectrum) ** 2 + jnp.imag(spectrum) ** 2))
    filtered = jnp.fft.ifft(green_k * spectrum, axis=1) * jnp.conj(phases)[:, :, None]
    potential = jnp.real(jnp.fft.ifft(jnp.fft.ifft(filtered, axis=0), axis=2))

    def read_step(sampled, offset_id):
        cell_x, cell_y, cell_z, weight_x, weight_y, weight_z = image_cells(offset_id)
        sample = potential[cell_x, cell_y, cell_z]
        products = jnp.stack([weight_x[p] * weight_y[r] * weight_z[s] for p, r, s in combos])
        return sampled + products * sample[None, :], None

    sampled, _ = lax.scan(read_step, jnp.zeros((10, ATOMS), jnp.float32), offset_ids)
    charge_grad = live * sampled[0]
    dipole_grad = live[None, :] * sampled[1:4]
    force_x = charge_live * sampled[1] + dipole_live[0] * sampled[4] + dipole_live[1] * sampled[7] + dipole_live[2] * sampled[8]
    force_y = charge_live * sampled[2] + dipole_live[0] * sampled[7] + dipole_live[1] * sampled[5] + dipole_live[2] * sampled[9]
    force_z = charge_live * sampled[3] + dipole_live[0] * sampled[8] + dipole_live[1] * sampled[9] + dipole_live[2] * sampled[6]
    position_grad = live[None, :] * jnp.stack([force_x, force_y, force_z])
    return charge_grad, dipole_grad, position_grad, jnp.reshape(energy, (1,))
```

```python
import functools
import math

import jax
import jax.numpy as jnp
import ml_dtypes
import numpy as np
from jax import lax
from jax.experimental import pallas as pl
from jax.experimental.pallas import tpu as pltpu
from jax.sharding import PartitionSpec as P

NX = 384
NZ = 360
CY = 6
LANES = 128
UNIT_X = 32
WIN = 40
EXT = NX + 8
SCREENING = 0.9
MESH = pl.DeviceIdType.MESH
F32 = jnp.float32
BF16 = jnp.bfloat16
VMEM_LIMIT = 52 * 1024 * 1024


def spline_tables(fraction):
    levels = {2: [1.0 - fraction, fraction]}
    current = levels[2]
    for n in range(3, 7):
        inverse_n = 1.0 / (n - 1)
        updated = [None] * n
        updated[n - 1] = inverse_n * fraction * current[n - 2]
        for j in range(1, n - 1):
            updated[n - 1 - j] = inverse_n * (
                (fraction + j) * current[n - 2 - j] + (n - j - fraction) * current[n - 1 - j]
            )
        updated[0] = inverse_n * (1.0 - fraction) * current[0]
        current = updated
        levels[n] = current
    zero_row = jnp.zeros_like(fraction)

    def entry_at(values_list, k):
        return values_list[k] if 0 <= k < len(values_list) else zero_row

    first = [entry_at(levels[5], t - 1) - entry_at(levels[5], t) for t in range(6)]
    second = [
        entry_at(levels[4], t - 2) - 2.0 * entry_at(levels[4], t - 1) + entry_at(levels[4], t)
        for t in range(6)
    ]
    return [levels[6], first, second]


def split_np(table):
    high = table.astype(np.float32).astype(ml_dtypes.bfloat16)
    low = (table - high.astype(np.float64)).astype(np.float32).astype(ml_dtypes.bfloat16)
    return high, low


def split(x):
    high = x.astype(BF16)
    return high, (x - high.astype(F32)).astype(BF16)


NN = (((1,), (0,)), ((), ()))
NT = (((1,), (1,)), ((), ()))
CHUNKS = ((0, 256), (256, 128))


def dot(left, right, dims):
    return lax.dot_general(left, right, dims, preferred_element_type=F32)


def dot3(left, right_high, right_low, dims):
    m = left.shape[0] // 2
    both = dot(left, right_high, dims)
    return both[:m] + (both[m:] + dot(left[:m], right_low, dims))


def stacked(x):
    return jnp.concatenate(split(x), axis=0)


def x_tables():
    ticks = np.outer(np.arange(NX), np.arange(NX)) % NX
    angles = 2.0 * np.pi / NX * ticks
    return np.concatenate([np.cos(angles), -np.sin(angles)], axis=0)


def y_tables(groups, kzp, rows_pad):
    ny = CY * groups
    ticks = np.outer(np.arange(ny), np.arange(ny)) % ny
    angles = 2.0 * np.pi / ny * ticks
    cos, sin = np.cos(angles), np.sin(angles)
    table = np.zeros((2, kzp, ny, groups, rows_pad))
    for k in range(kzp):
        for y in range(CY):
            at_y = np.arange(groups) * CY + y
            for c in range(2):
                row = (c * CY + y) * kzp + k
                if c == 0:
                    table[0, k, :, :, row] = cos[:, at_y]
                    table[1, k, :, :, row] = -sin[:, at_y]
                else:
                    table[0, k, :, :, row] = sin[:, at_y]
                    table[1, k, :, :, row] = cos[:, at_y]
    return table.reshape(2 * ny * kzp, groups * rows_pad)


def my_group(groups, pencils):
    flat = lax.axis_index("gy") * pencils + lax.axis_index("gx")
    return flat // groups, lax.rem(flat, groups)


def place(groups, pencils, g, s):
    flat = g * groups + s
    return flat // pencils, lax.rem(flat, pencils)


def ring_targets(groups, pencils, g, s):
    flat = g * groups + s
    home, pencil = flat // pencils, lax.rem(flat, pencils)
    found = []
    for v in range(2):
        for other in range(pencils):
            found.append((other, lax.rem(home + v, groups), v * pencils + pencil))
    return found


def ring_sources(groups, pencils, g, s):
    found = []
    for v in range(2):
        for j in range(pencils):
            flat = lax.rem(s - v + groups, groups) * pencils + j
            found.append((flat // groups, lax.rem(flat, groups), v * pencils + j))
    return found


def turn(ticks, period):
    quarter = jnp.floor(ticks * (4.0 / period) + 0.5)
    x = (ticks - (period / 4.0) * quarter) * (2.0 * math.pi / period)
    quarter = quarter - 4.0 * jnp.floor(quarter * 0.25)
    x2 = x * x
    sin = x + x * x2 * (
        -1.0 / 6.0 + x2 * (1.0 / 120.0 + x2 * (-1.0 / 5040.0 + x2 * (1.0 / 362880.0)))
    )
    cos = 1.0 + x2 * (
        -0.5 + x2 * (1.0 / 24.0 + x2 * (-1.0 / 720.0 + x2 * (1.0 / 40320.0)))
    )
    odd = (quarter == 1.0) | (quarter == 3.0)
    first, second = jnp.where(odd, sin, cos), jnp.where(odd, cos, sin)
    first = jnp.where((quarter == 1.0) | (quarter == 2.0), -first, first)
    second = jnp.where(quarter >= 2.0, -second, second)
    return first, second


def modulus(cos):
    return (64.0 + 52.0 * cos + 4.0 * cos * cos) * (1.0 / 120.0)


def dense_rows(tables, row, base, rows):
    index = lax.broadcasted_iota(jnp.int32, (rows, LANES), 0).astype(F32) - base
    at = [index == float(t) for t in range(6)]
    found = []
    for order in range(3):
        total = jnp.zeros((rows, LANES), F32)
        for t in range(6):
            total = jnp.where(at[t], tables[order][t][row : row + 1], total)
        found.append(total)
    return found


def mode_weights(tables, cell_z, kz, step_ref):
    cell_cos, cell_sin = turn(kz * cell_z, float(NZ))
    found = []
    for order in range(3):
        fc, fs = 0.0, 0.0
        for t in range(6):
            weight = tables[order][t][2:3]
            fc = fc + weight * step_ref[2 * t]
            fs = fs + weight * step_ref[2 * t + 1]
        found.append(
            jnp.concatenate(
                [cell_cos * fc - cell_sin * fs, cell_sin * fc + cell_cos * fs], axis=0
            )
        )
    return found


def fill_phases(phase_ref, s, groups, shear):
    ny = CY * groups
    shape = (2 * CY, NX)
    row = lax.broadcasted_iota(jnp.int32, shape, 0)
    col = lax.broadcasted_iota(jnp.int32, shape, 1)
    kx = jnp.where(col < NX // 2, col, col - NX)
    wrap = jnp.where(s == 0, ny, 0)
    y = s * CY + jnp.where(row < CY, row, row - CY + wrap)
    ticks = y * shear * kx
    period = NX * ny
    count = jnp.floor(ticks.astype(F32) * (1.0 / period)).astype(jnp.int32)
    cos, sin = turn((ticks - count * period).astype(F32), float(period))
    phase_ref[0] = cos
    phase_ref[1] = sin


def fill_green(gtab_ref, g, s, groups, kz_part, kzp, shear):
    ny = CY * groups
    shape = (ny, NX)
    row = lax.broadcasted_iota(jnp.int32, shape, 0)
    col = lax.broadcasted_iota(jnp.int32, shape, 1)
    kx = jnp.where(col < NX // 2, col, col - NX)
    ky = jnp.where(row < ny // 2, row, row - ny)
    fx, fy = kx.astype(F32), ky.astype(F32)
    wave = fy + fx * shear.astype(F32) * (1.0 / NX)
    plane = (fx * (1.0 / NX)) * (fx * (1.0 / NX)) + (wave * (1.0 / ny)) * (wave * (1.0 / ny))
    rate = -((math.pi / SCREENING) ** 2)
    cos_w, _ = turn((ky * NX + kx * shear).astype(F32), float(NX * ny))
    cos_x, _ = turn(fx, float(NX))
    mod_xy = modulus(cos_w) * modulus(cos_x)
    edge = (kx == -(NX // 2)) | (ky == -(ny // 2))
    front = jnp.where(edge, 0.0, jnp.exp(rate * plane) / (math.pi * mod_xy * mod_xy))
    origin = (kx == 0) & (ky == 0)
    for i in range(kzp):
        local = s * kzp + i
        kz = g * kz_part + local
        fz = jnp.full((1, NX), kz.astype(F32), F32)
        part_z = (fz * (1.0 / NZ)) * (fz * (1.0 / NZ))
        cos_z, _ = turn(fz, float(NZ))
        mod_z = modulus(cos_z)
        weight = jnp.where(fz == 0.0, 1.0, 2.0) * (1.0 / (NX * ny * NZ))
        used = (local < kz_part) & (kz < NZ // 2)
        front_z = jnp.where(used, weight * jnp.exp(rate * part_z) / (mod_z * mod_z), 0.0)
        zero = origin & (fz == 0.0)
        norm = jnp.where(zero, 1.0, plane + part_z)
        gtab_ref[i * ny : (i + 1) * ny] = jnp.where(zero, 0.0, front * front_z / norm)


def whole_kernel(
    groups, pencils, per_pencil, blocks, kz_part, kzt, kzp, rows_pad,
    cell_ref, off_ref, charge_ref, dip_ref, count_ref, shear_ref,
    cf_high_hbm, cf_low_hbm, c_hbm, w1_hbm, w2_hbm,
    out_ref,
    cf_high, cf_low, c_both, w1_both, w2_both,
    own, gathered, weights, z_high, z_low, cells, lhs, rhs_high, rhs_low,
    send, arrived, filtered, back, gtab_ref, phase_ref, step_ref, shares, parts, held,
    const_sem, get_send, get_recv, out_send, out_recv, back_send, back_recv,
    told_send, told_recv, ret_send, ret_recv,
):
    g, s = my_group(groups, pencils)
    ny = CY * groups
    zr = 2 * kzt
    modes = ny * kzp
    shear = shear_ref[0]
    targets = ring_targets(groups, pencils, g, s)
    sources = ring_sources(groups, pencils, g, s)
    peers = [lax.rem(s + k, groups) for k in range(1, groups)]

    barrier = pltpu.get_barrier_semaphore()
    for pg, ps, _ in sources + targets:
        pl.semaphore_signal(
            barrier, inc=1, device_id=place(groups, pencils, pg, ps), device_id_type=MESH
        )
    for p in peers:
        pl.semaphore_signal(
            barrier, inc=1, device_id=place(groups, pencils, g, p), device_id_type=MESH
        )

    loads = [
        pltpu.make_async_copy(source, target, const_sem.at[i])
        for i, (source, target) in enumerate(
            [
                (cf_high_hbm, cf_high),
                (cf_low_hbm, cf_low),
                (w1_hbm, w1_both),
                (w2_hbm, w2_both),
                (c_hbm, c_both),
            ]
        )
    ]
    for load in loads:
        load.start()

    atoms = own.shape[1]
    per_block = atoms // blocks
    lane = lax.broadcasted_iota(jnp.int32, (1, atoms), 1)
    live = jnp.zeros((1, atoms), F32)
    for b in range(blocks):
        first = b * per_block
        live = jnp.where((lane >= first) & (lane < first + count_ref[b]), 1.0, live)
    own[...] = jnp.concatenate(
        [
            cell_ref[...].astype(F32),
            off_ref[...],
            charge_ref[...] * live,
            dip_ref[...] * live,
            jnp.zeros((6, atoms), F32),
        ],
        axis=0,
    )
    pl.semaphore_wait(barrier, len(sources) + len(targets) + len(peers))

    def get_copy(i, pg, ps, slot):
        return pltpu.make_async_remote_copy(
            src_ref=own,
            dst_ref=gathered.at[slot],
            send_sem=get_send.at[i],
            recv_sem=get_recv.at[slot],
            device_id=place(groups, pencils, pg, ps),
            device_id_type=MESH,
        )

    for i, (pg, ps, slot) in enumerate(targets):
        here = (pg == g) & (ps == s)

        @pl.when(jnp.logical_not(here))
        def _():
            get_copy(i, pg, ps, slot).start()

        @pl.when(here)
        def _():
            gathered[slot] = own[...]

    fill_phases(phase_ref, s, groups, shear)
    fill_green(gtab_ref, g, s, groups, kz_part, kzp, shear)
    kz = (lax.broadcasted_iota(jnp.int32, (kzt, LANES), 0) + g * kz_part).astype(F32)
    for t in range(6):
        cos, sin = turn(kz * float(t), float(NZ))
        step_ref[2 * t] = cos
        step_ref[2 * t + 1] = sin
    cells[...] = jnp.zeros_like(cells)
    used = 2 * CY * kzp
    if rows_pad > used:
        for p in range(groups):
            send[p, used:rows_pad] = jnp.zeros((rows_pad - used, NX), F32)

    for pg, ps, slot in sources:
        here = (pg == g) & (ps == s)

        @pl.when(jnp.logical_not(here))
        def _():
            get_copy(0, pg, ps, slot).wait_recv()

    slab_low = lax.rem(s - 1 + groups, groups)
    y_base = [(s * CY).astype(F32), (slab_low * CY + CY).astype(F32)]

    def spread(j, carry):
        for k in range(per_pencil):
            x_at = pl.multiple_of((j * per_pencil + k) * UNIT_X, UNIT_X)
            x_base = x_at.astype(F32)
            for v in range(2):
                unit = (j * 2 + v) * per_pencil + k
                atom = gathered[v * pencils + j, :, k * LANES : (k + 1) * LANES]
                tables = spline_tables(atom[3:6])
                wx = dense_rows(tables, 0, atom[0:1] - x_base, WIN)
                wy = dense_rows(tables, 1, atom[1:2] - y_base[v], 8)
                z0, z1, z2 = mode_weights(tables, atom[2:3], kz, step_ref)
                weights[unit] = jnp.concatenate(wx + wy, axis=0)
                high, low = split(jnp.concatenate([z0, z1, z2], axis=1))
                z_high[unit] = high
                z_low[unit] = low
                q, mx, my, mz = (atom[i : i + 1] for i in range(6, 10))
                right = jnp.concatenate([q * z0 + mz * z1, z0], axis=1)
                mux_x = mx * wx[1]
                muy_x = my * wx[0]
                left = jnp.concatenate(
                    [
                        jnp.concatenate(
                            [
                                wy[0][y : y + 1] * wx[0],
                                wy[0][y : y + 1] * mux_x + wy[1][y : y + 1] * muy_x,
                            ],
                            axis=1,
                        )
                        for y in range(CY)
                    ],
                    axis=0,
                )
                part = dot3(stacked(left), *split(right), NT)
                for y in range(CY):
                    here = cells.at[v * CY + y, pl.ds(x_at, WIN), pl.ds(0, zr)]
                    here[...] = here[...] + part[y * WIN : (y + 1) * WIN]
        return carry

    lax.fori_loop(0, pencils, spread, 0)

    total = 2 * CY * zr
    for at in range(2 * CY):
        cells[at, 0:8] = cells[at, 0:8] + cells[at, NX:EXT]
        turned = jnp.transpose(cells[at, 0:NX])
        cos_part, sin_part = turned[0:kzt], turned[kzt:zr]
        high, low = split(
            jnp.concatenate(
                [
                    jnp.concatenate([cos_part, sin_part], axis=1),
                    jnp.concatenate([-sin_part, cos_part], axis=1),
                ],
                axis=0,
            )
        )
        lhs[at * zr : (at + 1) * zr] = high
        lhs[total + at * zr : total + (at + 1) * zr] = low

    def chunk_copies(source, target, send_sems, recv_sems, chunk):
        first, count = CHUNKS[chunk]
        return [
            pltpu.make_async_remote_copy(
                src_ref=source.at[p, :, pl.ds(first, count)],
                dst_ref=target.at[s, :, pl.ds(first, count)],
                send_sem=send_sems.at[chunk, k],
                recv_sem=recv_sems.at[chunk, k],
                device_id=place(groups, pencils, g, p),
                device_id_type=MESH,
            )
            for k, p in enumerate(peers)
        ]

    loads[0].wait()
    loads[1].wait()
    sent = []
    for chunk, (first, count) in enumerate(CHUNKS):
        cols = slice(first, first + count)
        lines = dot3(lhs[...], cf_high[:, cols], cf_low[:, cols], NN)
        for y in range(CY):
            real, imag = 0.0, 0.0
            for v in range(2):
                at = v * CY + y
                ct, st = phase_ref[0, at : at + 1, cols], phase_ref[1, at : at + 1, cols]
                re = lines[at * zr : at * zr + kzt]
                im = lines[at * zr + kzt : (at + 1) * zr]
                real = real + (re * ct + im * st)
                imag = imag + (im * ct - re * st)
            for c, values in enumerate((real, imag)):
                row = (c * CY + y) * kzp
                for p in range(groups):
                    send[p, row : row + kzp, cols] = values[p * kzp : (p + 1) * kzp]
        copies = chunk_copies(send, arrived, out_send, out_recv, chunk)
        for copy in copies:
            copy.start()
        arrived[s, :, cols] = send[s, :, cols]
        sent.append(copies)

    loads[2].wait()
    loads[3].wait()
    returned = []
    power = jnp.zeros((8, LANES), F32)
    flat = groups * rows_pad
    for chunk, (first, count) in enumerate(CHUNKS):
        cols = slice(first, first + count)
        for copy in sent[chunk]:
            copy.wait_recv()
        high, low = split(arrived[:, :, cols].reshape(flat, count))
        spectrum = dot3(w1_both[...], high, low, NN)
        real, imag = spectrum[:modes], spectrum[modes:]
        gtab = gtab_ref[:, cols]
        amount = jnp.sum(
            (gtab * (real * real + imag * imag)).reshape(modes // 8, 8, count), axis=0
        )
        for i in range(0, count, LANES):
            power = power + amount[:, i : i + LANES]
        high, low = split(jnp.concatenate([gtab * real, gtab * imag], axis=0))
        filtered[:, :, cols] = dot3(w2_both[...], high, low, NN).reshape(groups, rows_pad, count)
        copies = chunk_copies(filtered, back, back_send, back_recv, chunk)
        for copy in copies:
            copy.start()
        back[s, :, cols] = filtered[s, :, cols]
        returned.append(copies)
    shares[s] = power
    told = [
        pltpu.make_async_remote_copy(
            src_ref=shares.at[s],
            dst_ref=shares.at[s],
            send_sem=told_send.at[k],
            recv_sem=told_recv.at[k],
            device_id=place(groups, pencils, g, p),
            device_id_type=MESH,
        )
        for k, p in enumerate(peers)
    ]
    for copy in told:
        copy.start()

    loads[4].wait()
    for chunk, (first, count) in enumerate(CHUNKS):
        cols = slice(first, first + count)
        deep = slice(2 * first, 2 * (first + count))
        for copy in returned[chunk]:
            copy.wait_recv()
        for y in range(CY):
            found = []
            for c in range(2):
                row = (c * CY + y) * kzp
                found.append(
                    jnp.concatenate(
                        [back[p, row : row + kzp, cols] for p in range(groups)], axis=0
                    )
                )
            real, imag = found
            for v in range(2):
                at = v * CY + y
                ct, st = phase_ref[0, at : at + 1, cols], phase_ref[1, at : at + 1, cols]
                pr = real * ct - imag * st
                pi = imag * ct + real * st
                rows = [
                    jnp.concatenate([pr, pi], axis=1),
                    jnp.concatenate([-pi, pr], axis=1),
                ]
                if zr < LANES:
                    rows.append(jnp.zeros((LANES - zr, 2 * count), F32))
                high, low = split(jnp.concatenate(rows, axis=0))
                rhs_high[at * LANES : (at + 1) * LANES, deep] = high
                rhs_low[at * LANES : (at + 1) * LANES, deep] = low
        for pair in range(CY):
            at = pair * 2 * LANES
            found = dot3(
                c_both[:, deep],
                rhs_high[at : at + 2 * LANES, deep],
                rhs_low[at : at + 2 * LANES, deep],
                NT,
            )
            for half in range(2):
                here = cells.at[2 * pair + half, 0:NX]
                part = found[:, half * LANES : (half + 1) * LANES]
                here[...] = part if chunk == 0 else here[...] + part
    for at in range(2 * CY):
        cells[at, NX:EXT] = cells[at, 0:8]

    for copy in told:
        copy.wait_recv()
    share = jnp.sum(jnp.sum(shares[...], axis=0), axis=0, keepdims=True)
    share = jnp.broadcast_to(0.25 * jnp.sum(share, axis=1, keepdims=True), (1, LANES))

    def return_copy(slot, to_slot, pg, ps):
        return pltpu.make_async_remote_copy(
            src_ref=parts.at[slot],
            dst_ref=held.at[to_slot],
            send_sem=ret_send.at[slot],
            recv_sem=ret_recv.at[to_slot],
            device_id=place(groups, pencils, pg, ps),
            device_id_type=MESH,
        )

    def sample(j, carry):
        for k in range(per_pencil):
            x_at = pl.multiple_of((j * per_pencil + k) * UNIT_X, UNIT_X)
            for v in range(2):
                unit = (j * 2 + v) * per_pencil + k
                slot = v * pencils + j
                left = jnp.concatenate(
                    [cells[v * CY + y, pl.ds(x_at, WIN), pl.ds(0, zr)] for y in range(CY)],
                    axis=0,
                )
                proj = dot3(stacked(left), z_high[unit], z_low[unit], NN)
                wx = [weights[unit, o * WIN : (o + 1) * WIN] for o in range(3)]
                wy = [weights[unit, 3 * WIN + o * 8 : 3 * WIN + (o + 1) * 8] for o in range(3)]

                def over_y(r, order):
                    return sum(
                        wy[r][y : y + 1]
                        * proj[y * WIN : (y + 1) * WIN, order * LANES : (order + 1) * LANES]
                        for y in range(CY)
                    )

                def over_x(p, values):
                    return jnp.sum(wx[p] * values, axis=0, keepdims=True)

                q00, q10, q01 = over_y(0, 0), over_y(1, 0), over_y(0, 1)
                s000, s100, s200 = over_x(0, q00), over_x(1, q00), over_x(2, q00)
                s010, s110 = over_x(0, q10), over_x(1, q10)
                s001, s101 = over_x(0, q01), over_x(1, q01)
                s020 = over_x(0, over_y(2, 0))
                s002 = over_x(0, over_y(0, 2))
                s011 = over_x(0, over_y(1, 1))
                atom = gathered[slot, :, k * LANES : (k + 1) * LANES]
                q, mx, my, mz = (atom[i : i + 1] for i in range(6, 10))
                parts[slot, :, k * LANES : (k + 1) * LANES] = jnp.concatenate(
                    [
                        s000,
                        s100,
                        s010,
                        s001,
                        q * s100 + mx * s200 + my * s110 + mz * s101,
                        q * s010 + mx * s110 + my * s020 + mz * s011,
                        q * s001 + mx * s101 + my * s011 + mz * s002,
                        share,
                    ],
                    axis=0,
                )
        return carry

    lax.fori_loop(0, pencils, sample, 0)

    for i, (pg, ps, _) in enumerate(sources):
        here = (pg == g) & (ps == s)
        to_slot = (i // pencils) * pencils + g

        @pl.when(jnp.logical_not(here))
        def _():
            return_copy(i, to_slot, pg, ps).start()

        @pl.when(here)
        def _():
            held[to_slot] = parts[i]

    for i, (pg, ps, _) in enumerate(targets):
        here = (pg == g) & (ps == s)

        @pl.when(jnp.logical_not(here))
        def _():
            return_copy(0, i, pg, ps).wait_recv()

    summed = held[0]
    for i in range(1, 2 * pencils):
        summed = summed + held[i]
    row = lax.broadcasted_iota(jnp.int32, summed.shape, 0)
    out_ref[...] = jnp.where(row < 7, summed * live, summed)

    for copies in sent + returned + [told]:
        for copy in copies:
            copy.wait_send()
    for i, (pg, ps, slot) in enumerate(targets):
        here = (pg == g) & (ps == s)

        @pl.when(jnp.logical_not(here))
        def _():
            get_copy(i, pg, ps, slot).wait_send()

    for i, (pg, ps, _) in enumerate(sources):
        here = (pg == g) & (ps == s)

        @pl.when(jnp.logical_not(here))
        def _():
            return_copy(i, 0, pg, ps).wait_send()


def on_device(groups, pencils, cell_index, offsets, charges, dipoles, block_count, shear_cells):
    atoms = charges.shape[0]
    blocks = block_count.shape[0]
    per_pencil = atoms // LANES
    units = per_pencil * pencils
    ny = CY * groups
    kz_part = -(-(NZ // 2) // pencils)
    kzp = -(-kz_part // groups)
    kzt = kzp * groups
    zr = 2 * kzt
    rows_pad = -(-2 * CY * kzp // 8) * 8
    slots = 2 * pencils

    forward = x_tables()
    backward = np.concatenate(
        [forward[half : half + NX].T[:, a : a + n] for a, n in CHUNKS for half in (0, NX)], axis=1
    )
    y_table = y_tables(groups, kzp, rows_pad)
    cf_high, cf_low = split_np(forward)
    constants = [cf_high, cf_low] + [
        np.concatenate(split_np(table), axis=0)
        for table in (backward, y_table, np.ascontiguousarray(y_table.T))
    ]
    vmem = pl.BlockSpec(memory_space=pltpu.VMEM)
    smem = pl.BlockSpec(memory_space=pltpu.SMEM)
    block = (groups, rows_pad, NX)
    peers = (groups - 1,)
    sem = pltpu.SemaphoreType.DMA
    result = pl.pallas_call(
        functools.partial(
            whole_kernel, groups, pencils, per_pencil, blocks, kz_part, kzt, kzp, rows_pad
        ),
        out_shape=jax.ShapeDtypeStruct((8, atoms), F32),
        in_specs=[vmem] * 4 + [smem] * 2 + [pl.BlockSpec(memory_space=pl.ANY)] * 5,
        out_specs=vmem,
        scratch_shapes=[
            pltpu.VMEM((2 * NX, NX), BF16),
            pltpu.VMEM((2 * NX, NX), BF16),
            pltpu.VMEM((2 * NX, 2 * NX), BF16),
            pltpu.VMEM((4 * ny * kzp, groups * rows_pad), BF16),
            pltpu.VMEM((2 * groups * rows_pad, 2 * ny * kzp), BF16),
            pltpu.VMEM((16, atoms), F32),
            pltpu.VMEM((slots, 16, atoms), F32),
            pltpu.VMEM((2 * units, 3 * WIN + 24, LANES), F32),
            pltpu.VMEM((2 * units, zr, 3 * LANES), BF16),
            pltpu.VMEM((2 * units, zr, 3 * LANES), BF16),
            pltpu.VMEM((2 * CY, EXT, LANES), F32),
            pltpu.VMEM((4 * CY * zr, 2 * NX), BF16),
            pltpu.VMEM((2 * CY * LANES, 2 * NX), BF16),
            pltpu.VMEM((2 * CY * LANES, 2 * NX), BF16),
            pltpu.VMEM(block, F32),
            pltpu.VMEM(block, F32),
            pltpu.VMEM(block, F32),
            pltpu.VMEM(block, F32),
            pltpu.VMEM((ny * kzp, NX), F32),
            pltpu.VMEM((2, 2 * CY, NX), F32),
            pltpu.VMEM((12, kzt, LANES), F32),
            pltpu.VMEM((groups, 8, LANES), F32),
            pltpu.VMEM((slots, 8, atoms), F32),
            pltpu.VMEM((slots, 8, atoms), F32),
            sem((5,)),
            sem((slots,)),
            sem((slots,)),
            sem((2,) + peers),
            sem((2,) + peers),
            sem((2,) + peers),
            sem((2,) + peers),
            sem(peers),
            sem(peers),
            sem((slots,)),
            sem((slots,)),
        ],
        compiler_params=pltpu.CompilerParams(
            collective_id=0, has_side_effects=True, vmem_limit_bytes=VMEM_LIMIT
        ),
        name="ewald",
    )(
        cell_index,
        offsets,
        charges.reshape(1, atoms),
        dipoles,
        block_count,
        shear_cells,
        *[
            jnp.asarray(t)
            for t in (constants[0], constants[1], constants[2], constants[3], constants[4])
        ],
    )
    return result[0], result[1:4], result[4:7], result[7, 0:1]


def solution(mesh):
    groups, pencils = mesh.shape["gy"], mesh.shape["gx"]
    split_all = ("gy", "gx")
    return jax.shard_map(
        functools.partial(on_device, groups, pencils),
        mesh=mesh,
        in_specs=(
            P(None, split_all),
            P(None, split_all),
            P(split_all),
            P(None, split_all),
            P(split_all),
            P(),
        ),
        out_specs=(P(split_all), P(None, split_all), P(None, split_all), P()),
        check_vma=False,
    )
```

```python
import functools
import math

import jax
import jax.numpy as jnp
import ml_dtypes
import numpy as np
from jax import lax
from jax.experimental import pallas as pl
from jax.experimental.pallas import tpu as pltpu
from jax.sharding import PartitionSpec as P

NX = 384
NZ = 360
CY = 6
LANES = 128
ROWS = 2 * CY - 1
UNIT_X = 32
WIN = 40
EXT = NX + 8
SCREENING = 0.9
MESH = pl.DeviceIdType.MESH
F32 = jnp.float32
BF16 = jnp.bfloat16
VMEM_LIMIT = 63 * 1024 * 1024


def spline_tables(fraction):
    levels = {2: [1.0 - fraction, fraction]}
    current = levels[2]
    for n in range(3, 7):
        inverse_n = 1.0 / (n - 1)
        updated = [None] * n
        updated[n - 1] = inverse_n * fraction * current[n - 2]
        for j in range(1, n - 1):
            updated[n - 1 - j] = inverse_n * (
                (fraction + j) * current[n - 2 - j] + (n - j - fraction) * current[n - 1 - j]
            )
        updated[0] = inverse_n * (1.0 - fraction) * current[0]
        current = updated
        levels[n] = current
    zero_row = jnp.zeros_like(fraction)

    def entry_at(values_list, k):
        return values_list[k] if 0 <= k < len(values_list) else zero_row

    first = [entry_at(levels[5], t - 1) - entry_at(levels[5], t) for t in range(6)]
    second = [
        entry_at(levels[4], t - 2) - 2.0 * entry_at(levels[4], t - 1) + entry_at(levels[4], t)
        for t in range(6)
    ]
    return [levels[6], first, second]


def split_np(table):
    high = table.astype(np.float32).astype(ml_dtypes.bfloat16)
    low = (table - high.astype(np.float64)).astype(np.float32).astype(ml_dtypes.bfloat16)
    return high, low


def split(x):
    high = x.astype(BF16)
    return high, (x - high.astype(F32)).astype(BF16)


NN = (((1,), (0,)), ((), ()))
NT = (((1,), (1,)), ((), ()))
CHUNKS = ((0, 256), (256, 128))


def dot(left, right, dims):
    return lax.dot_general(left, right, dims, preferred_element_type=F32)


def dot3(left, right_high, right_low, dims):
    m = left.shape[0] // 2
    both = dot(left, right_high, dims)
    return both[:m] + (both[m:] + dot(left[:m], right_low, dims))


def stacked(x):
    return jnp.concatenate(split(x), axis=0)


def x_tables():
    ticks = np.outer(np.arange(NX), np.arange(NX)) % NX
    angles = 2.0 * np.pi / NX * ticks
    return np.concatenate([np.cos(angles), -np.sin(angles)], axis=0)


def y_tables(groups, kzp, rows_pad):
    ny = CY * groups
    ticks = np.outer(np.arange(ny), np.arange(ny)) % ny
    angles = 2.0 * np.pi / ny * ticks
    cos, sin = np.cos(angles), np.sin(angles)
    table = np.zeros((2, kzp, ny, groups, rows_pad))
    for k in range(kzp):
        for y in range(CY):
            at_y = np.arange(groups) * CY + y
            for c in range(2):
                row = (c * CY + y) * kzp + k
                if c == 0:
                    table[0, k, :, :, row] = cos[:, at_y]
                    table[1, k, :, :, row] = -sin[:, at_y]
                else:
                    table[0, k, :, :, row] = sin[:, at_y]
                    table[1, k, :, :, row] = cos[:, at_y]
    return table.reshape(2 * ny * kzp, groups * rows_pad)


def my_group(groups, pencils):
    flat = lax.axis_index("gy") * pencils + lax.axis_index("gx")
    return flat // groups, lax.rem(flat, groups)


def place(groups, pencils, g, s):
    flat = g * groups + s
    return flat // pencils, lax.rem(flat, pencils)


def ring_targets(groups, pencils, g, s):
    flat = g * groups + s
    home, pencil = flat // pencils, lax.rem(flat, pencils)
    found = []
    for v in range(2):
        for other in range(pencils):
            found.append((other, lax.rem(home + v, groups), v * pencils + pencil))
    return found


def ring_sources(groups, pencils, g, s):
    found = []
    for v in range(2):
        for j in range(pencils):
            flat = lax.rem(s - v + groups, groups) * pencils + j
            found.append((flat // groups, lax.rem(flat, groups), v * pencils + j))
    return found


def turn(ticks, period):
    quarter = jnp.floor(ticks * (4.0 / period) + 0.5)
    x = (ticks - (period / 4.0) * quarter) * (2.0 * math.pi / period)
    quarter = quarter - 4.0 * jnp.floor(quarter * 0.25)
    x2 = x * x
    sin = x + x * x2 * (
        -1.0 / 6.0 + x2 * (1.0 / 120.0 + x2 * (-1.0 / 5040.0 + x2 * (1.0 / 362880.0)))
    )
    cos = 1.0 + x2 * (
        -0.5 + x2 * (1.0 / 24.0 + x2 * (-1.0 / 720.0 + x2 * (1.0 / 40320.0)))
    )
    odd = (quarter == 1.0) | (quarter == 3.0)
    first, second = jnp.where(odd, sin, cos), jnp.where(odd, cos, sin)
    first = jnp.where((quarter == 1.0) | (quarter == 2.0), -first, first)
    second = jnp.where(quarter >= 2.0, -second, second)
    return first, second


def modulus(cos):
    return (64.0 + 52.0 * cos + 4.0 * cos * cos) * (1.0 / 120.0)


def dense_rows(tables, row, base, rows):
    index = lax.broadcasted_iota(jnp.int32, (rows, LANES), 0).astype(F32) - base
    at = [index == float(t) for t in range(6)]
    found = []
    for order in range(3):
        total = jnp.zeros((rows, LANES), F32)
        for t in range(6):
            total = jnp.where(at[t], tables[order][t][row : row + 1], total)
        found.append(total)
    return found


def mode_weights(tables, cell_z, kz, step_ref):
    cell_cos, cell_sin = turn(kz * cell_z, float(NZ))
    found = []
    for order in range(3):
        fc, fs = 0.0, 0.0
        for t in range(6):
            weight = tables[order][t][2:3]
            fc = fc + weight * step_ref[2 * t]
            fs = fs + weight * step_ref[2 * t + 1]
        found.append(
            jnp.concatenate(
                [cell_cos * fc - cell_sin * fs, cell_sin * fc + cell_cos * fs], axis=0
            )
        )
    return found


def fill_phases(phase_ref, s, groups, shear):
    ny = CY * groups
    shape = (2 * CY, NX)
    row = lax.broadcasted_iota(jnp.int32, shape, 0)
    col = lax.broadcasted_iota(jnp.int32, shape, 1)
    kx = jnp.where(col < NX // 2, col, col - NX)
    wrap = jnp.where(s == 0, ny, 0)
    y = s * CY + jnp.where(row < CY, row, row - CY + wrap)
    ticks = y * shear * kx
    period = NX * ny
    count = jnp.floor(ticks.astype(F32) * (1.0 / period)).astype(jnp.int32)
    cos, sin = turn((ticks - count * period).astype(F32), float(period))
    phase_ref[0] = cos
    phase_ref[1] = sin


def fill_green(gtab_ref, g, s, groups, kz_part, kzp, shear):
    ny = CY * groups
    shape = (ny, NX)
    row = lax.broadcasted_iota(jnp.int32, shape, 0)
    col = lax.broadcasted_iota(jnp.int32, shape, 1)
    kx = jnp.where(col < NX // 2, col, col - NX)
    ky = jnp.where(row < ny // 2, row, row - ny)
    fx, fy = kx.astype(F32), ky.astype(F32)
    wave = fy + fx * shear.astype(F32) * (1.0 / NX)
    plane = (fx * (1.0 / NX)) * (fx * (1.0 / NX)) + (wave * (1.0 / ny)) * (wave * (1.0 / ny))
    rate = -((math.pi / SCREENING) ** 2)
    cos_w, _ = turn((ky * NX + kx * shear).astype(F32), float(NX * ny))
    cos_x, _ = turn(fx, float(NX))
    mod_xy = modulus(cos_w) * modulus(cos_x)
    edge = (kx == -(NX // 2)) | (ky == -(ny // 2))
    front = jnp.where(edge, 0.0, jnp.exp(rate * plane) / (math.pi * mod_xy * mod_xy))
    origin = (kx == 0) & (ky == 0)
    for i in range(kzp):
        local = s * kzp + i
        kz = g * kz_part + local
        fz = jnp.full((1, NX), kz.astype(F32), F32)
        part_z = (fz * (1.0 / NZ)) * (fz * (1.0 / NZ))
        cos_z, _ = turn(fz, float(NZ))
        mod_z = modulus(cos_z)
        weight = jnp.where(fz == 0.0, 1.0, 2.0) * (1.0 / (NX * ny * NZ))
        used = (local < kz_part) & (kz < NZ // 2)
        front_z = jnp.where(used, weight * jnp.exp(rate * part_z) / (mod_z * mod_z), 0.0)
        zero = origin & (fz == 0.0)
        norm = jnp.where(zero, 1.0, plane + part_z)
        gtab_ref[i * ny : (i + 1) * ny] = jnp.where(zero, 0.0, front * front_z / norm)


def whole_kernel(
    groups, pencils, per_pencil, blocks, kz_part, kzt, kzp, rows_pad,
    cell_hbm, off_hbm, charge_hbm, dip_hbm, count_hbm, shear_hbm,
    cf_high_hbm, cf_low_hbm, c_hbm, w1_hbm, w2_hbm,
    out_ref,
    cell_ref, off_ref, charge_ref, dip_ref, count_ref, shear_ref,
    cf_high, cf_low, c_both, w1_both, w2_both,
    own, gathered, weights, z_high, z_low, cells, lhs, rhs_high, rhs_low,
    send, arrived, filtered, back, gtab_ref, phase_ref, step_ref, shares, parts, held,
    input_sem, const_sem, get_send, get_recv, out_send, out_recv, back_send, back_recv,
    told_send, told_recv, ret_send, ret_recv,
):
    g, s = my_group(groups, pencils)
    ny = CY * groups
    zr = 2 * kzt
    modes = ny * kzp
    inputs = [
        pltpu.make_async_copy(source, target, input_sem.at[i])
        for i, (source, target) in enumerate(
            [
                (cell_hbm, cell_ref),
                (off_hbm, off_ref),
                (charge_hbm, charge_ref),
                (dip_hbm, dip_ref),
                (count_hbm, count_ref),
                (shear_hbm, shear_ref),
            ]
        )
    ]
    for load in inputs:
        load.start()
    targets = ring_targets(groups, pencils, g, s)
    sources = ring_sources(groups, pencils, g, s)
    peers = [lax.rem(s + k, groups) for k in range(1, groups)]

    barrier = pltpu.get_barrier_semaphore()
    for pg, ps, _ in sources + targets:
        pl.semaphore_signal(
            barrier, inc=1, device_id=place(groups, pencils, pg, ps), device_id_type=MESH
        )
    for p in peers:
        pl.semaphore_signal(
            barrier, inc=1, device_id=place(groups, pencils, g, p), device_id_type=MESH
        )

    loads = [
        pltpu.make_async_copy(source, target, const_sem.at[i])
        for i, (source, target) in enumerate(
            [
                (cf_high_hbm, cf_high),
                (cf_low_hbm, cf_low),
                (w1_hbm, w1_both),
                (w2_hbm, w2_both),
                (c_hbm, c_both),
            ]
        )
    ]
    for load in loads:
        load.start()

    for load in inputs:
        load.wait()
    shear = shear_ref[0]
    atoms = out_ref.shape[1]
    per_block = atoms // blocks
    lane = lax.broadcasted_iota(jnp.int32, (1, atoms), 1)
    live = jnp.zeros((1, atoms), F32)
    for b in range(blocks):
        first = b * per_block
        live = jnp.where((lane >= first) & (lane < first + count_ref[b]), 1.0, live)
    told_rows = jnp.concatenate(
        [
            cell_ref[...].astype(F32),
            off_ref[...],
            charge_ref[...].reshape(1, atoms) * live,
            dip_ref[...] * live,
        ],
        axis=0,
    )
    own[...] = jnp.zeros_like(own)
    for k in range(per_pencil):
        own[k * 10 : (k + 1) * 10] = told_rows[:, k * LANES : (k + 1) * LANES]
    pl.semaphore_wait(barrier, len(sources) + len(targets) + len(peers))

    def get_copy(i, pg, ps, slot):
        return pltpu.make_async_remote_copy(
            src_ref=own,
            dst_ref=gathered.at[slot],
            send_sem=get_send.at[i],
            recv_sem=get_recv.at[slot],
            device_id=place(groups, pencils, pg, ps),
            device_id_type=MESH,
        )

    for i, (pg, ps, slot) in enumerate(targets):
        here = (pg == g) & (ps == s)

        @pl.when(jnp.logical_not(here))
        def _():
            get_copy(i, pg, ps, slot).start()

        @pl.when(here)
        def _():
            gathered[slot] = own[...]

    fill_phases(phase_ref, s, groups, shear)
    fill_green(gtab_ref, g, s, groups, kz_part, kzp, shear)
    kz = (lax.broadcasted_iota(jnp.int32, (kzt, LANES), 0) + g * kz_part).astype(F32)
    for t in range(6):
        cos, sin = turn(kz * float(t), float(NZ))
        step_ref[2 * t] = cos
        step_ref[2 * t + 1] = sin
    cells[...] = jnp.zeros_like(cells)
    used = 2 * CY * kzp
    if rows_pad > used:
        for p in range(groups):
            send[p, used:rows_pad] = jnp.zeros((rows_pad - used, NX), F32)

    def source_of(v, j):
        flat = lax.rem(s - v + groups, groups) * pencils + j
        pg, ps = flat // groups, lax.rem(flat, groups)
        return pg, ps, (pg == g) & (ps == s)

    slab_low = lax.rem(s - 1 + groups, groups)
    y_base = [(s * CY).astype(F32), (slab_low * CY + CY).astype(F32)]

    def spread(j, carry):
        for v in range(2):
            pg, ps, here = source_of(v, j)

            @pl.when(jnp.logical_not(here))
            def _():
                get_copy(0, pg, ps, v * pencils + j).wait_recv()

        for k in range(per_pencil):
            x_at = pl.multiple_of((j * per_pencil + k) * UNIT_X, UNIT_X)
            x_base = x_at.astype(F32)
            for v in range(2):
                unit = (j * 2 + v) * per_pencil + k
                atom = gathered[v * pencils + j, k * 10 : (k + 1) * 10]
                tables = spline_tables(atom[3:6])
                wx = dense_rows(tables, 0, atom[0:1] - x_base, WIN)
                wy = dense_rows(tables, 1, atom[1:2] - y_base[v], 8)
                z0, z1, z2 = mode_weights(tables, atom[2:3], kz, step_ref)
                weights[unit] = jnp.concatenate(wx + wy, axis=0)
                z_all = [jnp.concatenate([z0, z1, z2], axis=1)]
                if zr < LANES:
                    z_all.append(jnp.zeros((LANES - zr, 3 * LANES), F32))
                high, low = split(jnp.concatenate(z_all, axis=0))
                z_high[unit] = high
                z_low[unit] = low
                q, mx, my, mz = (atom[i : i + 1] for i in range(6, 10))
                right = jnp.concatenate([q * z0 + mz * z1, z0], axis=1)
                mux_x = mx * wx[1]
                muy_x = my * wx[0]
                left = jnp.concatenate(
                    [
                        jnp.concatenate(
                            [
                                wy[0][y : y + 1] * wx[0],
                                wy[0][y : y + 1] * mux_x + wy[1][y : y + 1] * muy_x,
                            ],
                            axis=1,
                        )
                        for y in range(CY - v)
                    ],
                    axis=0,
                )
                part = dot3(stacked(left), *split(right), NT)
                for y in range(CY - v):
                    here = cells.at[v * CY + y, pl.ds(x_at, WIN), pl.ds(0, zr)]
                    here[...] = here[...] + part[y * WIN : (y + 1) * WIN]
        return carry

    lax.fori_loop(0, pencils, spread, 0)

    total = ROWS * zr
    for at in range(ROWS):
        cells[at, 0:8] = cells[at, 0:8] + cells[at, NX:EXT]
        turned = jnp.transpose(cells[at, 0:NX])
        cos_part, sin_part = turned[0:kzt], turned[kzt:zr]
        high, low = split(
            jnp.concatenate(
                [
                    jnp.concatenate([cos_part, sin_part], axis=1),
                    jnp.concatenate([-sin_part, cos_part], axis=1),
                ],
                axis=0,
            )
        )
        lhs[at * zr : (at + 1) * zr] = high
        lhs[total + at * zr : total + (at + 1) * zr] = low

    def chunk_copies(source, target, send_sems, recv_sems, chunk):
        first, count = CHUNKS[chunk]
        return [
            pltpu.make_async_remote_copy(
                src_ref=source.at[p, :, pl.ds(first, count)],
                dst_ref=target.at[s, :, pl.ds(first, count)],
                send_sem=send_sems.at[chunk, k],
                recv_sem=recv_sems.at[chunk, k],
                device_id=place(groups, pencils, g, p),
                device_id_type=MESH,
            )
            for k, p in enumerate(peers)
        ]

    loads[0].wait()
    loads[1].wait()
    sent = []
    for chunk, (first, count) in enumerate(CHUNKS):
        cols = slice(first, first + count)
        lines = dot3(lhs[...], cf_high[:, cols], cf_low[:, cols], NN)
        for y in range(CY):
            real, imag = 0.0, 0.0
            for v in range(2 if y < CY - 1 else 1):
                at = v * CY + y
                ct, st = phase_ref[0, at : at + 1, cols], phase_ref[1, at : at + 1, cols]
                re = lines[at * zr : at * zr + kzt]
                im = lines[at * zr + kzt : (at + 1) * zr]
                real = real + (re * ct + im * st)
                imag = imag + (im * ct - re * st)
            for c, values in enumerate((real, imag)):
                row = (c * CY + y) * kzp
                for p in range(groups):
                    send[p, row : row + kzp, cols] = values[p * kzp : (p + 1) * kzp]
        copies = chunk_copies(send, arrived, out_send, out_recv, chunk)
        for copy in copies:
            copy.start()
        arrived[s, :, cols] = send[s, :, cols]
        sent.append(copies)

    loads[2].wait()
    loads[3].wait()
    returned = []
    power = jnp.zeros((8, LANES), F32)
    flat = groups * rows_pad
    for chunk, (first, count) in enumerate(CHUNKS):
        cols = slice(first, first + count)
        for copy in sent[chunk]:
            copy.wait_recv()
        high, low = split(arrived[:, :, cols].reshape(flat, count))
        spectrum = dot3(w1_both[...], high, low, NN)
        real, imag = spectrum[:modes], spectrum[modes:]
        gtab = gtab_ref[:, cols]
        amount = jnp.sum(
            (gtab * (real * real + imag * imag)).reshape(modes // 8, 8, count), axis=0
        )
        for i in range(0, count, LANES):
            power = power + amount[:, i : i + LANES]
        high, low = split(jnp.concatenate([gtab * real, gtab * imag], axis=0))
        filtered[:, :, cols] = dot3(w2_both[...], high, low, NN).reshape(groups, rows_pad, count)
        copies = chunk_copies(filtered, back, back_send, back_recv, chunk)
        for copy in copies:
            copy.start()
        back[s, :, cols] = filtered[s, :, cols]
        returned.append(copies)
    shares[s] = power
    told = [
        pltpu.make_async_remote_copy(
            src_ref=shares.at[s],
            dst_ref=shares.at[s],
            send_sem=told_send.at[k],
            recv_sem=told_recv.at[k],
            device_id=place(groups, pencils, g, p),
            device_id_type=MESH,
        )
        for k, p in enumerate(peers)
    ]
    for copy in told:
        copy.start()

    loads[4].wait()
    for chunk, (first, count) in enumerate(CHUNKS):
        cols = slice(first, first + count)
        deep = slice(2 * first, 2 * (first + count))
        for copy in returned[chunk]:
            copy.wait_recv()
        for y in range(CY):
            found = []
            for c in range(2):
                row = (c * CY + y) * kzp
                found.append(
                    jnp.concatenate(
                        [back[p, row : row + kzp, cols] for p in range(groups)], axis=0
                    )
                )
            real, imag = found
            for v in range(2 if y < CY - 1 else 1):
                at = v * CY + y
                ct, st = phase_ref[0, at : at + 1, cols], phase_ref[1, at : at + 1, cols]
                pr = real * ct - imag * st
                pi = imag * ct + real * st
                rows = [
                    jnp.concatenate([pr, pi], axis=1),
                    jnp.concatenate([-pi, pr], axis=1),
                ]
                if zr < LANES:
                    rows.append(jnp.zeros((LANES - zr, 2 * count), F32))
                high, low = split(jnp.concatenate(rows, axis=0))
                rhs_high[at * LANES : (at + 1) * LANES, deep] = high
                rhs_low[at * LANES : (at + 1) * LANES, deep] = low
        for pair in range(0, ROWS, 2):
            many = min(2, ROWS - pair)
            at = slice(pair * LANES, (pair + many) * LANES)
            found = dot3(c_both[:, deep], rhs_high[at, deep], rhs_low[at, deep], NT)
            for half in range(many):
                here = cells.at[pair + half, 0:NX]
                part = found[:, half * LANES : (half + 1) * LANES]
                here[...] = part if chunk == 0 else here[...] + part
    for at in range(ROWS):
        cells[at, NX:EXT] = cells[at, 0:8]

    for copy in told:
        copy.wait_recv()
    share = jnp.sum(jnp.sum(shares[...], axis=0), axis=0, keepdims=True)
    share = jnp.broadcast_to(0.25 * jnp.sum(share, axis=1, keepdims=True), (1, LANES))

    def return_copy(slot, to_slot, pg, ps):
        return pltpu.make_async_remote_copy(
            src_ref=parts.at[slot],
            dst_ref=held.at[to_slot],
            send_sem=ret_send.at[slot],
            recv_sem=ret_recv.at[to_slot],
            device_id=place(groups, pencils, pg, ps),
            device_id_type=MESH,
        )

    def sample(j, carry):
        for k in range(per_pencil):
            x_at = pl.multiple_of((j * per_pencil + k) * UNIT_X, UNIT_X)
            for v in range(2):
                unit = (j * 2 + v) * per_pencil + k
                slot = v * pencils + j
                left = jnp.concatenate(
                    [cells[v * CY + y, pl.ds(x_at, WIN)] for y in range(CY - v)], axis=0
                )
                high, low = split(left)
                z_now = z_high[unit]
                proj = dot(
                    jnp.concatenate([high, low], axis=1),
                    jnp.concatenate([z_now, z_now], axis=0),
                    NN,
                ) + dot(high, z_low[unit], NN)
                wx = [weights[unit, o * WIN : (o + 1) * WIN] for o in range(3)]
                wy = [weights[unit, 3 * WIN + o * 8 : 3 * WIN + (o + 1) * 8] for o in range(3)]

                def over_y(r, order):
                    return sum(
                        wy[r][y : y + 1]
                        * proj[y * WIN : (y + 1) * WIN, order * LANES : (order + 1) * LANES]
                        for y in range(CY - v)
                    )

                def over_x(p, values):
                    return jnp.sum(wx[p] * values, axis=0, keepdims=True)

                q00, q10, q01 = over_y(0, 0), over_y(1, 0), over_y(0, 1)
                s000, s100, s200 = over_x(0, q00), over_x(1, q00), over_x(2, q00)
                s010, s110 = over_x(0, q10), over_x(1, q10)
                s001, s101 = over_x(0, q01), over_x(1, q01)
                s020 = over_x(0, over_y(2, 0))
                s002 = over_x(0, over_y(0, 2))
                s011 = over_x(0, over_y(1, 1))
                atom = gathered[slot, k * 10 : (k + 1) * 10]
                q, mx, my, mz = (atom[i : i + 1] for i in range(6, 10))
                parts[slot, :, k * LANES : (k + 1) * LANES] = jnp.concatenate(
                    [
                        s000,
                        s100,
                        s010,
                        s001,
                        q * s100 + mx * s200 + my * s110 + mz * s101,
                        q * s010 + mx * s110 + my * s020 + mz * s011,
                        q * s001 + mx * s101 + my * s011 + mz * s002,
                        share,
                    ],
                    axis=0,
                )
        for v in range(2):
            slot, to_slot = v * pencils + j, v * pencils + g
            pg, ps, here = source_of(v, j)

            @pl.when(jnp.logical_not(here))
            def _():
                return_copy(slot, to_slot, pg, ps).start()

            @pl.when(here)
            def _():
                held[to_slot] = parts[slot]

        return carry

    lax.fori_loop(0, pencils, sample, 0)

    for i, (pg, ps, _) in enumerate(targets):
        here = (pg == g) & (ps == s)

        @pl.when(jnp.logical_not(here))
        def _():
            return_copy(0, i, pg, ps).wait_recv()

    summed = held[0]
    for i in range(1, 2 * pencils):
        summed = summed + held[i]
    row = lax.broadcasted_iota(jnp.int32, summed.shape, 0)
    out_ref[...] = jnp.where(row < 7, summed * live, summed)

    for copies in sent + returned + [told]:
        for copy in copies:
            copy.wait_send()
    for i, (pg, ps, slot) in enumerate(targets):
        here = (pg == g) & (ps == s)

        @pl.when(jnp.logical_not(here))
        def _():
            get_copy(i, pg, ps, slot).wait_send()

    for i, (pg, ps, _) in enumerate(sources):
        here = (pg == g) & (ps == s)

        @pl.when(jnp.logical_not(here))
        def _():
            return_copy(i, 0, pg, ps).wait_send()


def on_device(groups, pencils, cell_index, offsets, charges, dipoles, block_count, shear_cells):
    atoms = charges.shape[0]
    blocks = block_count.shape[0]
    per_pencil = atoms // LANES
    units = per_pencil * pencils
    ny = CY * groups
    kz_part = -(-(NZ // 2) // pencils)
    kzp = -(-kz_part // groups)
    kzt = kzp * groups
    zr = 2 * kzt
    rows_pad = -(-2 * CY * kzp // 8) * 8
    slots = 2 * pencils
    told = -(-10 * per_pencil // 8) * 8

    forward = x_tables()
    backward = np.concatenate(
        [forward[half : half + NX].T[:, a : a + n] for a, n in CHUNKS for half in (0, NX)], axis=1
    )
    y_table = y_tables(groups, kzp, rows_pad)
    cf_high, cf_low = split_np(forward)
    constants = [cf_high, cf_low] + [
        np.concatenate(split_np(table), axis=0)
        for table in (backward, y_table, np.ascontiguousarray(y_table.T))
    ]
    vmem = pl.BlockSpec(memory_space=pltpu.VMEM)
    block = (groups, rows_pad, NX)
    peers = (groups - 1,)
    sem = pltpu.SemaphoreType.DMA
    result = pl.pallas_call(
        functools.partial(
            whole_kernel, groups, pencils, per_pencil, blocks, kz_part, kzt, kzp, rows_pad
        ),
        out_shape=jax.ShapeDtypeStruct((8, atoms), F32),
        in_specs=[pl.BlockSpec(memory_space=pl.ANY)] * 11,
        out_specs=vmem,
        scratch_shapes=[
            pltpu.VMEM(cell_index.shape, jnp.int32),
            pltpu.VMEM(offsets.shape, F32),
            pltpu.VMEM(charges.shape, F32),
            pltpu.VMEM(dipoles.shape, F32),
            pltpu.SMEM(block_count.shape, jnp.int32),
            pltpu.SMEM(shear_cells.shape, jnp.int32),
            pltpu.VMEM((2 * NX, NX), BF16),
            pltpu.VMEM((2 * NX, NX), BF16),
            pltpu.VMEM((2 * NX, 2 * NX), BF16),
            pltpu.VMEM((4 * ny * kzp, groups * rows_pad), BF16),
            pltpu.VMEM((2 * groups * rows_pad, 2 * ny * kzp), BF16),
            pltpu.VMEM((told, LANES), F32),
            pltpu.VMEM((slots, told, LANES), F32),
            pltpu.VMEM((2 * units, 3 * WIN + 24, LANES), F32),
            pltpu.VMEM((2 * units, LANES, 3 * LANES), BF16),
            pltpu.VMEM((2 * units, LANES, 3 * LANES), BF16),
            pltpu.VMEM((ROWS, EXT, LANES), F32),
            pltpu.VMEM((2 * ROWS * zr, 2 * NX), BF16),
            pltpu.VMEM((ROWS * LANES, 2 * NX), BF16),
            pltpu.VMEM((ROWS * LANES, 2 * NX), BF16),
            pltpu.VMEM(block, F32),
            pltpu.VMEM(block, F32),
            pltpu.VMEM(block, F32),
            pltpu.VMEM(block, F32),
            pltpu.VMEM((ny * kzp, NX), F32),
            pltpu.VMEM((2, 2 * CY, NX), F32),
            pltpu.VMEM((12, kzt, LANES), F32),
            pltpu.VMEM((groups, 8, LANES), F32),
            pltpu.VMEM((slots, 8, atoms), F32),
            pltpu.VMEM((slots, 8, atoms), F32),
            sem((6,)),
            sem((5,)),
            sem((slots,)),
            sem((slots,)),
            sem((2,) + peers),
            sem((2,) + peers),
            sem((2,) + peers),
            sem((2,) + peers),
            sem(peers),
            sem(peers),
            sem((slots,)),
            sem((slots,)),
        ],
        compiler_params=pltpu.CompilerParams(
            collective_id=0, has_side_effects=True, vmem_limit_bytes=VMEM_LIMIT
        ),
        name="ewald",
    )(
        cell_index,
        offsets,
        charges,
        dipoles,
        block_count,
        shear_cells,
        *[
            jnp.asarray(t)
            for t in (constants[0], constants[1], constants[2], constants[3], constants[4])
        ],
    )
    return result[0], result[1:4], result[4:7], result[7, 0:1]


def solution(mesh):
    groups, pencils = mesh.shape["gy"], mesh.shape["gx"]
    split_all = ("gy", "gx")
    return jax.shard_map(
        functools.partial(on_device, groups, pencils),
        mesh=mesh,
        in_specs=(
            P(None, split_all),
            P(None, split_all),
            P(split_all),
            P(None, split_all),
            P(split_all),
            P(),
        ),
        out_specs=(P(split_all), P(None, split_all), P(None, split_all), P()),
        check_vma=False,
    )
```

```python
import functools
import math

import jax
import jax.numpy as jnp
import ml_dtypes
import numpy as np
from jax import lax
from jax.experimental import pallas as pl
from jax.experimental.pallas import tpu as pltpu
from jax.sharding import PartitionSpec as P

NX = 384
NZ = 360
CY = 6
LANES = 128
ROWS = 2 * CY - 1
UNIT_X = 32
WIN = 40
EXT = NX + 8
SCREENING = 0.9
MESH = pl.DeviceIdType.MESH
F32 = jnp.float32
BF16 = jnp.bfloat16
VMEM_LIMIT = 63 * 1024 * 1024


def spline_tables(fraction):
    levels = {2: [1.0 - fraction, fraction]}
    current = levels[2]
    for n in range(3, 7):
        inverse_n = 1.0 / (n - 1)
        updated = [None] * n
        updated[n - 1] = inverse_n * fraction * current[n - 2]
        for j in range(1, n - 1):
            updated[n - 1 - j] = inverse_n * (
                (fraction + j) * current[n - 2 - j] + (n - j - fraction) * current[n - 1 - j]
            )
        updated[0] = inverse_n * (1.0 - fraction) * current[0]
        current = updated
        levels[n] = current
    zero_row = jnp.zeros_like(fraction)

    def entry_at(values_list, k):
        return values_list[k] if 0 <= k < len(values_list) else zero_row

    first = [entry_at(levels[5], t - 1) - entry_at(levels[5], t) for t in range(6)]
    second = [
        entry_at(levels[4], t - 2) - 2.0 * entry_at(levels[4], t - 1) + entry_at(levels[4], t)
        for t in range(6)
    ]
    return [levels[6], first, second]


def split_np(table):
    high = table.astype(np.float32).astype(ml_dtypes.bfloat16)
    low = (table - high.astype(np.float64)).astype(np.float32).astype(ml_dtypes.bfloat16)
    return high, low


def split(x):
    high = x.astype(BF16)
    return high, (x - high.astype(F32)).astype(BF16)


NN = (((1,), (0,)), ((), ()))
NT = (((1,), (1,)), ((), ()))
CHUNKS = ((0, 256), (256, 128))


def dot(left, right, dims):
    return lax.dot_general(left, right, dims, preferred_element_type=F32)


def dot3(left, right_high, right_low, dims):
    m = left.shape[0] // 2
    both = dot(left, right_high, dims)
    return both[:m] + (both[m:] + dot(left[:m], right_low, dims))


def dot_wide(left, right_high, right_low, dims):
    k = left.shape[1] // 2
    twice = jnp.concatenate([right_high, right_high], axis=0)
    return dot(left, twice, dims) + dot(left[:, :k], right_low, dims)


def stacked(x):
    return jnp.concatenate(split(x), axis=0)


def x_tables():
    ticks = np.outer(np.arange(NX), np.arange(NX)) % NX
    angles = 2.0 * np.pi / NX * ticks
    return np.concatenate([np.cos(angles), -np.sin(angles)], axis=0)


def y_tables(groups, kzp, rows_pad):
    ny = CY * groups
    ticks = np.outer(np.arange(ny), np.arange(ny)) % ny
    angles = 2.0 * np.pi / ny * ticks
    cos, sin = np.cos(angles), np.sin(angles)
    table = np.zeros((2, kzp, ny, groups, rows_pad))
    for k in range(kzp):
        for y in range(CY):
            at_y = np.arange(groups) * CY + y
            for c in range(2):
                row = (c * CY + y) * kzp + k
                if c == 0:
                    table[0, k, :, :, row] = cos[:, at_y]
                    table[1, k, :, :, row] = -sin[:, at_y]
                else:
                    table[0, k, :, :, row] = sin[:, at_y]
                    table[1, k, :, :, row] = cos[:, at_y]
    return table.reshape(2 * ny * kzp, groups * rows_pad)


def my_group(groups, pencils):
    flat = lax.axis_index("gy") * pencils + lax.axis_index("gx")
    return flat // groups, lax.rem(flat, groups)


def place(groups, pencils, g, s):
    flat = g * groups + s
    return flat // pencils, lax.rem(flat, pencils)


def ring_targets(groups, pencils, g, s):
    flat = g * groups + s
    home, pencil = flat // pencils, lax.rem(flat, pencils)
    found = []
    for v in range(2):
        for other in range(pencils):
            found.append((other, lax.rem(home + v, groups), v * pencils + pencil))
    return found


def ring_sources(groups, pencils, g, s):
    found = []
    for v in range(2):
        for j in range(pencils):
            flat = lax.rem(s - v + groups, groups) * pencils + j
            found.append((flat // groups, lax.rem(flat, groups), v * pencils + j))
    return found


def turn(ticks, period):
    quarter = jnp.floor(ticks * (4.0 / period) + 0.5)
    x = (ticks - (period / 4.0) * quarter) * (2.0 * math.pi / period)
    quarter = quarter - 4.0 * jnp.floor(quarter * 0.25)
    x2 = x * x
    sin = x + x * x2 * (
        -1.0 / 6.0 + x2 * (1.0 / 120.0 + x2 * (-1.0 / 5040.0 + x2 * (1.0 / 362880.0)))
    )
    cos = 1.0 + x2 * (
        -0.5 + x2 * (1.0 / 24.0 + x2 * (-1.0 / 720.0 + x2 * (1.0 / 40320.0)))
    )
    odd = (quarter == 1.0) | (quarter == 3.0)
    first, second = jnp.where(odd, sin, cos), jnp.where(odd, cos, sin)
    first = jnp.where((quarter == 1.0) | (quarter == 2.0), -first, first)
    second = jnp.where(quarter >= 2.0, -second, second)
    return first, second


def modulus(cos):
    return (64.0 + 52.0 * cos + 4.0 * cos * cos) * (1.0 / 120.0)


def dense_rows(tables, row, base, rows):
    index = lax.broadcasted_iota(jnp.int32, (rows, LANES), 0).astype(F32) - base
    at = [index == float(t) for t in range(6)]
    found = []
    for order in range(3):
        total = jnp.zeros((rows, LANES), F32)
        for t in range(6):
            total = jnp.where(at[t], tables[order][t][row : row + 1], total)
        found.append(total)
    return found


def mode_weights(tables, cell_z, kz, step_ref):
    cell_cos, cell_sin = turn(kz * cell_z, float(NZ))
    found = []
    for order in range(3):
        fc, fs = 0.0, 0.0
        for t in range(6):
            weight = tables[order][t][2:3]
            fc = fc + weight * step_ref[2 * t]
            fs = fs + weight * step_ref[2 * t + 1]
        found.append(
            jnp.concatenate(
                [cell_cos * fc - cell_sin * fs, cell_sin * fc + cell_cos * fs], axis=0
            )
        )
    return found


def fill_phases(phase_ref, s, groups, shear):
    ny = CY * groups
    shape = (2 * CY, NX)
    row = lax.broadcasted_iota(jnp.int32, shape, 0)
    col = lax.broadcasted_iota(jnp.int32, shape, 1)
    kx = jnp.where(col < NX // 2, col, col - NX)
    wrap = jnp.where(s == 0, ny, 0)
    y = s * CY + jnp.where(row < CY, row, row - CY + wrap)
    ticks = y * shear * kx
    period = NX * ny
    count = jnp.floor(ticks.astype(F32) * (1.0 / period)).astype(jnp.int32)
    cos, sin = turn((ticks - count * period).astype(F32), float(period))
    phase_ref[0] = cos
    phase_ref[1] = sin


def fill_green(gtab_ref, g, s, groups, kz_part, kzp, shear):
    ny = CY * groups
    shape = (ny, NX)
    row = lax.broadcasted_iota(jnp.int32, shape, 0)
    col = lax.broadcasted_iota(jnp.int32, shape, 1)
    kx = jnp.where(col < NX // 2, col, col - NX)
    ky = jnp.where(row < ny // 2, row, row - ny)
    fx, fy = kx.astype(F32), ky.astype(F32)
    wave = fy + fx * shear.astype(F32) * (1.0 / NX)
    plane = (fx * (1.0 / NX)) * (fx * (1.0 / NX)) + (wave * (1.0 / ny)) * (wave * (1.0 / ny))
    rate = -((math.pi / SCREENING) ** 2)
    cos_w, _ = turn((ky * NX + kx * shear).astype(F32), float(NX * ny))
    cos_x, _ = turn(fx, float(NX))
    mod_xy = modulus(cos_w) * modulus(cos_x)
    edge = (kx == -(NX // 2)) | (ky == -(ny // 2))
    front = jnp.where(edge, 0.0, jnp.exp(rate * plane) / (math.pi * mod_xy * mod_xy))
    origin = (kx == 0) & (ky == 0)
    for i in range(kzp):
        local = s * kzp + i
        kz = g * kz_part + local
        fz = jnp.full((1, NX), kz.astype(F32), F32)
        part_z = (fz * (1.0 / NZ)) * (fz * (1.0 / NZ))
        cos_z, _ = turn(fz, float(NZ))
        mod_z = modulus(cos_z)
        weight = jnp.where(fz == 0.0, 1.0, 2.0) * (1.0 / (NX * ny * NZ))
        used = (local < kz_part) & (kz < NZ // 2)
        front_z = jnp.where(used, weight * jnp.exp(rate * part_z) / (mod_z * mod_z), 0.0)
        zero = origin & (fz == 0.0)
        norm = jnp.where(zero, 1.0, plane + part_z)
        gtab_ref[i * ny : (i + 1) * ny] = jnp.where(zero, 0.0, front * front_z / norm)


def whole_kernel(
    groups, pencils, per_pencil, blocks, kz_part, kzt, kzp, rows_pad,
    cell_hbm, off_hbm, charge_hbm, dip_hbm, count_hbm, shear_hbm,
    cf_high_hbm, cf_low_hbm, c_hbm, w1_hbm, w2_hbm,
    out_ref,
    cell_ref, off_ref, charge_ref, dip_ref, count_ref, shear_ref,
    cf_high, cf_low, c_both, w1_both, w2_both,
    own, gathered, weights, z_high, z_low, cells, lhs, rhs_high, rhs_low,
    send, arrived, filtered, back, gtab_ref, phase_ref, step_ref, shares, parts, held,
    input_sem, const_sem, get_send, get_recv, out_send, out_recv, back_send, back_recv,
    told_send, told_recv, ret_send, ret_recv,
):
    g, s = my_group(groups, pencils)
    ny = CY * groups
    zr = 2 * kzt
    modes = ny * kzp
    inputs = [
        pltpu.make_async_copy(source, target, input_sem.at[i])
        for i, (source, target) in enumerate(
            [
                (cell_hbm, cell_ref),
                (off_hbm, off_ref),
                (charge_hbm, charge_ref),
                (dip_hbm, dip_ref),
                (count_hbm, count_ref),
                (shear_hbm, shear_ref),
            ]
        )
    ]
    for load in inputs:
        load.start()
    targets = ring_targets(groups, pencils, g, s)
    sources = ring_sources(groups, pencils, g, s)
    peers = [lax.rem(s + k, groups) for k in range(1, groups)]

    barrier = pltpu.get_barrier_semaphore()
    for pg, ps, _ in sources + targets:
        pl.semaphore_signal(
            barrier, inc=1, device_id=place(groups, pencils, pg, ps), device_id_type=MESH
        )
    for p in peers:
        pl.semaphore_signal(
            barrier, inc=1, device_id=place(groups, pencils, g, p), device_id_type=MESH
        )

    loads = [
        pltpu.make_async_copy(source, target, const_sem.at[i])
        for i, (source, target) in enumerate(
            [
                (cf_high_hbm, cf_high),
                (cf_low_hbm, cf_low),
                (w1_hbm, w1_both),
                (w2_hbm, w2_both),
                (c_hbm, c_both),
            ]
        )
    ]
    for load in loads:
        load.start()

    for load in inputs:
        load.wait()
    shear = shear_ref[0]
    atoms = out_ref.shape[1]
    per_block = atoms // blocks
    lane = lax.broadcasted_iota(jnp.int32, (1, atoms), 1)
    live = jnp.zeros((1, atoms), F32)
    for b in range(blocks):
        first = b * per_block
        live = jnp.where((lane >= first) & (lane < first + count_ref[b]), 1.0, live)
    told_rows = jnp.concatenate(
        [
            cell_ref[...].astype(F32),
            off_ref[...],
            charge_ref[...].reshape(1, atoms) * live,
            dip_ref[...] * live,
        ],
        axis=0,
    )
    own[...] = jnp.zeros_like(own)
    for k in range(per_pencil):
        own[k * 10 : (k + 1) * 10] = told_rows[:, k * LANES : (k + 1) * LANES]
    pl.semaphore_wait(barrier, len(sources) + len(targets) + len(peers))

    def get_copy(i, pg, ps, slot):
        return pltpu.make_async_remote_copy(
            src_ref=own,
            dst_ref=gathered.at[slot],
            send_sem=get_send.at[i],
            recv_sem=get_recv.at[slot],
            device_id=place(groups, pencils, pg, ps),
            device_id_type=MESH,
        )

    for i, (pg, ps, slot) in enumerate(targets):
        here = (pg == g) & (ps == s)

        @pl.when(jnp.logical_not(here))
        def _():
            get_copy(i, pg, ps, slot).start()

        @pl.when(here)
        def _():
            gathered[slot] = own[...]

    fill_phases(phase_ref, s, groups, shear)
    fill_green(gtab_ref, g, s, groups, kz_part, kzp, shear)
    kz = (lax.broadcasted_iota(jnp.int32, (kzt, LANES), 0) + g * kz_part).astype(F32)
    for t in range(6):
        cos, sin = turn(kz * float(t), float(NZ))
        step_ref[2 * t] = cos
        step_ref[2 * t + 1] = sin
    cells[...] = jnp.zeros_like(cells)
    used = 2 * CY * kzp
    if rows_pad > used:
        for p in range(groups):
            send[p, used:rows_pad] = jnp.zeros((rows_pad - used, NX), F32)

    def source_of(v, j):
        flat = lax.rem(s - v + groups, groups) * pencils + j
        pg, ps = flat // groups, lax.rem(flat, groups)
        return pg, ps, (pg == g) & (ps == s)

    slab_low = lax.rem(s - 1 + groups, groups)
    y_base = [(s * CY).astype(F32), (slab_low * CY + CY).astype(F32)]

    def spread(j, carry):
        for v in range(2):
            pg, ps, here = source_of(v, j)

            @pl.when(jnp.logical_not(here))
            def _():
                get_copy(0, pg, ps, v * pencils + j).wait_recv()

        for k in range(per_pencil):
            x_at = pl.multiple_of((j * per_pencil + k) * UNIT_X, UNIT_X)
            x_base = x_at.astype(F32)
            for v in range(2):
                unit = (j * 2 + v) * per_pencil + k
                atom = gathered[v * pencils + j, k * 10 : (k + 1) * 10]
                tables = spline_tables(atom[3:6])
                wx = dense_rows(tables, 0, atom[0:1] - x_base, WIN)
                wy = dense_rows(tables, 1, atom[1:2] - y_base[v], 8)
                z0, z1, z2 = mode_weights(tables, atom[2:3], kz, step_ref)
                weights[unit] = jnp.concatenate(wx + wy, axis=0)
                z_all = [jnp.concatenate([z0, z1, z2], axis=1)]
                if zr < LANES:
                    z_all.append(jnp.zeros((LANES - zr, 3 * LANES), F32))
                high, low = split(jnp.concatenate(z_all, axis=0))
                z_high[unit] = high
                z_low[unit] = low
                q, mx, my, mz = (atom[i : i + 1] for i in range(6, 10))
                right = jnp.concatenate([q * z0 + mz * z1, z0], axis=1)
                mux_x = mx * wx[1]
                muy_x = my * wx[0]
                left = jnp.concatenate(
                    [
                        jnp.concatenate(
                            [
                                wy[0][y : y + 1] * wx[0],
                                wy[0][y : y + 1] * mux_x + wy[1][y : y + 1] * muy_x,
                            ],
                            axis=1,
                        )
                        for y in range(CY - v)
                    ],
                    axis=0,
                )
                part = dot3(stacked(left), *split(right), NT)
                for y in range(CY - v):
                    here = cells.at[v * CY + y, pl.ds(x_at, WIN), pl.ds(0, zr)]
                    here[...] = here[...] + part[y * WIN : (y + 1) * WIN]
        return carry

    lax.fori_loop(0, pencils, spread, 0)

    for at in range(ROWS):
        cells[at, 0:8] = cells[at, 0:8] + cells[at, NX:EXT]
        turned = jnp.transpose(cells[at, 0:NX])
        cos_part, sin_part = turned[0:kzt], turned[kzt:zr]
        high, low = split(
            jnp.concatenate(
                [
                    jnp.concatenate([cos_part, sin_part], axis=1),
                    jnp.concatenate([-sin_part, cos_part], axis=1),
                ],
                axis=0,
            )
        )
        lhs[at * zr : (at + 1) * zr, 0 : 2 * NX] = high
        lhs[at * zr : (at + 1) * zr, 2 * NX : 4 * NX] = low

    def chunk_copies(source, target, send_sems, recv_sems, chunk):
        first, count = CHUNKS[chunk]
        return [
            pltpu.make_async_remote_copy(
                src_ref=source.at[p, :, pl.ds(first, count)],
                dst_ref=target.at[s, :, pl.ds(first, count)],
                send_sem=send_sems.at[chunk, k],
                recv_sem=recv_sems.at[chunk, k],
                device_id=place(groups, pencils, g, p),
                device_id_type=MESH,
            )
            for k, p in enumerate(peers)
        ]

    loads[0].wait()
    loads[1].wait()
    sent = []
    for chunk, (first, count) in enumerate(CHUNKS):
        cols = slice(first, first + count)
        lines = dot_wide(lhs[...], cf_high[:, cols], cf_low[:, cols], NN)
        for y in range(CY):
            real, imag = 0.0, 0.0
            for v in range(2 if y < CY - 1 else 1):
                at = v * CY + y
                ct, st = phase_ref[0, at : at + 1, cols], phase_ref[1, at : at + 1, cols]
                re = lines[at * zr : at * zr + kzt]
                im = lines[at * zr + kzt : (at + 1) * zr]
                real = real + (re * ct + im * st)
                imag = imag + (im * ct - re * st)
            for c, values in enumerate((real, imag)):
                row = (c * CY + y) * kzp
                for p in range(groups):
                    send[p, row : row + kzp, cols] = values[p * kzp : (p + 1) * kzp]
        copies = chunk_copies(send, arrived, out_send, out_recv, chunk)
        for copy in copies:
            copy.start()
        arrived[s, :, cols] = send[s, :, cols]
        sent.append(copies)

    loads[2].wait()
    loads[3].wait()
    returned = []
    power = jnp.zeros((8, LANES), F32)
    flat = groups * rows_pad
    for chunk, (first, count) in enumerate(CHUNKS):
        cols = slice(first, first + count)
        for copy in sent[chunk]:
            copy.wait_recv()
        high, low = split(arrived[:, :, cols].reshape(flat, count))
        spectrum = dot_wide(w1_both[...], high, low, NN)
        real, imag = spectrum[:modes], spectrum[modes:]
        gtab = gtab_ref[:, cols]
        amount = jnp.sum(
            (gtab * (real * real + imag * imag)).reshape(modes // 8, 8, count), axis=0
        )
        for i in range(0, count, LANES):
            power = power + amount[:, i : i + LANES]
        high, low = split(jnp.concatenate([gtab * real, gtab * imag], axis=0))
        filtered[:, :, cols] = dot_wide(w2_both[...], high, low, NN).reshape(groups, rows_pad, count)
        copies = chunk_copies(filtered, back, back_send, back_recv, chunk)
        for copy in copies:
            copy.start()
        back[s, :, cols] = filtered[s, :, cols]
        returned.append(copies)
    shares[s] = power
    told = [
        pltpu.make_async_remote_copy(
            src_ref=shares.at[s],
            dst_ref=shares.at[s],
            send_sem=told_send.at[k],
            recv_sem=told_recv.at[k],
            device_id=place(groups, pencils, g, p),
            device_id_type=MESH,
        )
        for k, p in enumerate(peers)
    ]
    for copy in told:
        copy.start()

    loads[4].wait()
    for chunk, (first, count) in enumerate(CHUNKS):
        cols = slice(first, first + count)
        deep = slice(2 * first, 2 * (first + count))
        for copy in returned[chunk]:
            copy.wait_recv()
        for y in range(CY):
            found = []
            for c in range(2):
                row = (c * CY + y) * kzp
                found.append(
                    jnp.concatenate(
                        [back[p, row : row + kzp, cols] for p in range(groups)], axis=0
                    )
                )
            real, imag = found
            for v in range(2 if y < CY - 1 else 1):
                at = v * CY + y
                ct, st = phase_ref[0, at : at + 1, cols], phase_ref[1, at : at + 1, cols]
                pr = real * ct - imag * st
                pi = imag * ct + real * st
                rows = [
                    jnp.concatenate([pr, pi], axis=1),
                    jnp.concatenate([-pi, pr], axis=1),
                ]
                if zr < LANES:
                    rows.append(jnp.zeros((LANES - zr, 2 * count), F32))
                high, low = split(jnp.concatenate(rows, axis=0))
                rhs_high[at * LANES : (at + 1) * LANES, deep] = high
                rhs_low[at * LANES : (at + 1) * LANES, deep] = low
        for pair in range(0, ROWS, 2):
            many = min(2, ROWS - pair)
            at = slice(pair * LANES, (pair + many) * LANES)
            found = dot3(c_both[:, deep], rhs_high[at, deep], rhs_low[at, deep], NT)
            for half in range(many):
                here = cells.at[pair + half, 0:NX]
                part = found[:, half * LANES : (half + 1) * LANES]
                here[...] = part if chunk == 0 else here[...] + part
    for at in range(ROWS):
        cells[at, NX:EXT] = cells[at, 0:8]

    for copy in told:
        copy.wait_recv()
    share = jnp.sum(jnp.sum(shares[...], axis=0), axis=0, keepdims=True)
    share = jnp.broadcast_to(0.25 * jnp.sum(share, axis=1, keepdims=True), (1, LANES))

    def return_copy(slot, to_slot, pg, ps):
        return pltpu.make_async_remote_copy(
            src_ref=parts.at[slot],
            dst_ref=held.at[to_slot],
            send_sem=ret_send.at[slot],
            recv_sem=ret_recv.at[to_slot],
            device_id=place(groups, pencils, pg, ps),
            device_id_type=MESH,
        )

    def sample(j, carry):
        for k in range(per_pencil):
            x_at = pl.multiple_of((j * per_pencil + k) * UNIT_X, UNIT_X)
            for v in range(2):
                unit = (j * 2 + v) * per_pencil + k
                slot = v * pencils + j
                left = jnp.concatenate(
                    [cells[v * CY + y, pl.ds(x_at, WIN)] for y in range(CY - v)], axis=0
                )
                high, low = split(left)
                z_now = z_high[unit]
                proj = dot(
                    jnp.concatenate([high, low], axis=1),
                    jnp.concatenate([z_now, z_now], axis=0),
                    NN,
                ) + dot(high, z_low[unit], NN)
                wx = [weights[unit, o * WIN : (o + 1) * WIN] for o in range(3)]
                wy = [weights[unit, 3 * WIN + o * 8 : 3 * WIN + (o + 1) * 8] for o in range(3)]

                def over_y(r, order):
                    return sum(
                        wy[r][y : y + 1]
                        * proj[y * WIN : (y + 1) * WIN, order * LANES : (order + 1) * LANES]
                        for y in range(CY - v)
                    )

                def over_x(p, values):
                    return jnp.sum(wx[p] * values, axis=0, keepdims=True)

                q00, q10, q01 = over_y(0, 0), over_y(1, 0), over_y(0, 1)
                s000, s100, s200 = over_x(0, q00), over_x(1, q00), over_x(2, q00)
                s010, s110 = over_x(0, q10), over_x(1, q10)
                s001, s101 = over_x(0, q01), over_x(1, q01)
                s020 = over_x(0, over_y(2, 0))
                s002 = over_x(0, over_y(0, 2))
                s011 = over_x(0, over_y(1, 1))
                atom = gathered[slot, k * 10 : (k + 1) * 10]
                q, mx, my, mz = (atom[i : i + 1] for i in range(6, 10))
                parts[slot, :, k * LANES : (k + 1) * LANES] = jnp.concatenate(
                    [
                        s000,
                        s100,
                        s010,
                        s001,
                        q * s100 + mx * s200 + my * s110 + mz * s101,
                        q * s010 + mx * s110 + my * s020 + mz * s011,
                        q * s001 + mx * s101 + my * s011 + mz * s002,
                        share,
                    ],
                    axis=0,
                )
        for v in range(2):
            slot, to_slot = v * pencils + j, v * pencils + g
            pg, ps, here = source_of(v, j)

            @pl.when(jnp.logical_not(here))
            def _():
                return_copy(slot, to_slot, pg, ps).start()

            @pl.when(here)
            def _():
                held[to_slot] = parts[slot]

        return carry

    lax.fori_loop(0, pencils, sample, 0)

    for i, (pg, ps, _) in enumerate(targets):
        here = (pg == g) & (ps == s)

        @pl.when(jnp.logical_not(here))
        def _():
            return_copy(0, i, pg, ps).wait_recv()

    summed = held[0]
    for i in range(1, 2 * pencils):
        summed = summed + held[i]
    row = lax.broadcasted_iota(jnp.int32, summed.shape, 0)
    out_ref[...] = jnp.where(row < 7, summed * live, summed)

    for copies in sent + returned + [told]:
        for copy in copies:
            copy.wait_send()
    for i, (pg, ps, slot) in enumerate(targets):
        here = (pg == g) & (ps == s)

        @pl.when(jnp.logical_not(here))
        def _():
            get_copy(i, pg, ps, slot).wait_send()

    for i, (pg, ps, _) in enumerate(sources):
        here = (pg == g) & (ps == s)

        @pl.when(jnp.logical_not(here))
        def _():
            return_copy(i, 0, pg, ps).wait_send()


def part_kernel(rows_ref, charge_ref, dipole_ref, position_ref, energy_ref):
    charge_ref[...] = rows_ref[0:1].reshape(charge_ref.shape)
    dipole_ref[...] = rows_ref[1:4]
    position_ref[...] = rows_ref[4:7]
    energy_ref[...] = rows_ref[7:8, 0:1]


def on_device(groups, pencils, cell_index, offsets, charges, dipoles, block_count, shear_cells):
    atoms = charges.shape[0]
    blocks = block_count.shape[0]
    per_pencil = atoms // LANES
    units = per_pencil * pencils
    ny = CY * groups
    kz_part = -(-(NZ // 2) // pencils)
    kzp = -(-kz_part // groups)
    kzt = kzp * groups
    zr = 2 * kzt
    rows_pad = -(-2 * CY * kzp // 8) * 8
    slots = 2 * pencils
    told = -(-10 * per_pencil // 8) * 8

    forward = x_tables()
    backward = np.concatenate(
        [forward[half : half + NX].T[:, a : a + n] for a, n in CHUNKS for half in (0, NX)], axis=1
    )
    y_table = y_tables(groups, kzp, rows_pad)
    cf_high, cf_low = split_np(forward)
    constants = [cf_high, cf_low, np.concatenate(split_np(backward), axis=0)] + [
        np.concatenate(split_np(table), axis=1)
        for table in (y_table, np.ascontiguousarray(y_table.T))
    ]
    vmem = pl.BlockSpec(memory_space=pltpu.VMEM)
    block = (groups, rows_pad, NX)
    peers = (groups - 1,)
    sem = pltpu.SemaphoreType.DMA
    result = pl.pallas_call(
        functools.partial(
            whole_kernel, groups, pencils, per_pencil, blocks, kz_part, kzt, kzp, rows_pad
        ),
        out_shape=jax.ShapeDtypeStruct((8, atoms), F32),
        in_specs=[pl.BlockSpec(memory_space=pl.ANY)] * 11,
        out_specs=vmem,
        scratch_shapes=[
            pltpu.VMEM(cell_index.shape, jnp.int32),
            pltpu.VMEM(offsets.shape, F32),
            pltpu.VMEM(charges.shape, F32),
            pltpu.VMEM(dipoles.shape, F32),
            pltpu.SMEM(block_count.shape, jnp.int32),
            pltpu.SMEM(shear_cells.shape, jnp.int32),
            pltpu.VMEM((2 * NX, NX), BF16),
            pltpu.VMEM((2 * NX, NX), BF16),
            pltpu.VMEM((2 * NX, 2 * NX), BF16),
            pltpu.VMEM((2 * ny * kzp, 2 * groups * rows_pad), BF16),
            pltpu.VMEM((groups * rows_pad, 4 * ny * kzp), BF16),
            pltpu.VMEM((told, LANES), F32),
            pltpu.VMEM((slots, told, LANES), F32),
            pltpu.VMEM((2 * units, 3 * WIN + 24, LANES), F32),
            pltpu.VMEM((2 * units, LANES, 3 * LANES), BF16),
            pltpu.VMEM((2 * units, LANES, 3 * LANES), BF16),
            pltpu.VMEM((ROWS, EXT, LANES), F32),
            pltpu.VMEM((ROWS * zr, 4 * NX), BF16),
            pltpu.VMEM((ROWS * LANES, 2 * NX), BF16),
            pltpu.VMEM((ROWS * LANES, 2 * NX), BF16),
            pltpu.VMEM(block, F32),
            pltpu.VMEM(block, F32),
            pltpu.VMEM(block, F32),
            pltpu.VMEM(block, F32),
            pltpu.VMEM((ny * kzp, NX), F32),
            pltpu.VMEM((2, 2 * CY, NX), F32),
            pltpu.VMEM((12, kzt, LANES), F32),
            pltpu.VMEM((groups, 8, LANES), F32),
            pltpu.VMEM((slots, 8, atoms), F32),
            pltpu.VMEM((slots, 8, atoms), F32),
            sem((6,)),
            sem((5,)),
            sem((slots,)),
            sem((slots,)),
            sem((2,) + peers),
            sem((2,) + peers),
            sem((2,) + peers),
            sem((2,) + peers),
            sem(peers),
            sem(peers),
            sem((slots,)),
            sem((slots,)),
        ],
        compiler_params=pltpu.CompilerParams(
            collective_id=0, has_side_effects=True, vmem_limit_bytes=VMEM_LIMIT
        ),
        name="ewald",
    )(
        cell_index,
        offsets,
        charges,
        dipoles,
        block_count,
        shear_cells,
        *[
            jnp.asarray(t)
            for t in (constants[0], constants[1], constants[2], constants[3], constants[4])
        ],
    )
    charge_grad, dipole_grad, position_grad, energy = pl.pallas_call(
        part_kernel,
        out_shape=(
            jax.ShapeDtypeStruct((atoms,), F32),
            jax.ShapeDtypeStruct((3, atoms), F32),
            jax.ShapeDtypeStruct((3, atoms), F32),
            jax.ShapeDtypeStruct((1, 1), F32),
        ),
        in_specs=[vmem],
        out_specs=(vmem,) * 4,
        name="part_outputs",
    )(result)
    return charge_grad, dipole_grad, position_grad, energy.reshape(1)


def solution(mesh):
    groups, pencils = mesh.shape["gy"], mesh.shape["gx"]
    split_all = ("gy", "gx")
    return jax.shard_map(
        functools.partial(on_device, groups, pencils),
        mesh=mesh,
        in_specs=(
            P(None, split_all),
            P(None, split_all),
            P(split_all),
            P(None, split_all),
            P(split_all),
            P(),
        ),
        out_specs=(P(split_all), P(None, split_all), P(None, split_all), P()),
        check_vma=False,
    )
```
